512 devices in a mesh: ta: 8 (over z_hi, core), ha: 8 (over y), wa: 8 (over z_lo, x).
Axes of the slice: x: 4, y: 8, z: 8 (z_hi: 4, z_lo: 2; z = z_hi * 2 + z_lo), core: 2. Of those that a mesh axis runs over, the one named last changes fastest.
Arguments:
- query_tokens: bfloat16 [8, 8, 384, 3072], P('ha', 'wa', 'ta'), may hold values from -5 to 5
- key_tokens: bfloat16 [8, 8, 384, 3072], P('ha', 'wa', 'ta'), may hold values from -5 to 5
- value_tokens: bfloat16 [8, 8, 384, 3072], P('ha', 'wa', 'ta'), may hold values from -5 to 5
- grad_output: bfloat16 [8, 8, 384, 3072], P('ha', 'wa', 'ta'), may hold values from -5 to 5
- windows: int32 [24, 2], replicated, may hold values from 1 to 3, as said below
Outputs:
- grad_queries: bfloat16 [8, 8, 384, 3072], P('ha', 'wa', 'ta')
- grad_keys: bfloat16 [8, 8, 384, 3072], P('ha', 'wa', 'ta')
- grad_values: bfloat16 [8, 8, 384, 3072], P('ha', 'wa', 'ta')
The draws below stay inside these ranges and needn't reach their ends.
Inputs may be any that keep to these rules, and one draw needn't show every extreme that they name: `windows`: every entry is 1 or 3; some head has 3 along both axes.
All inputs are finite; a program needn't handle non-finite values.
Results may differ from the reference program's by a relative error of at most 0.035.
Values may be sent and summed in bfloat16 or wider, within the bound.
No kernel may reach another device: no remote copies, remote signals or barrier semaphores. Data moves between devices by JAX's collectives and lax.ppermute only.
A program may use at most 128 MiB of HBM per device.

```python
import jax
import jax.numpy as jnp
import numpy as np
from jax import lax

HD = 128
HEADS = 24
TILE = 384
F = 3072
BH = 8
BW = 8


def draw_query_tokens(key, part):
    key = jax.random.fold_in(key, 11)
    base = jnp.clip(jax.random.normal(key, (BH, BW, TILE, F), jnp.float32), -5.0, 5.0)
    return base.astype(jnp.bfloat16)


def draw_key_tokens(key, part):
    key = jax.random.fold_in(key, 23)
    base = jnp.clip(jax.random.normal(key, (BH, BW, TILE, F), jnp.float32), -5.0, 5.0)
    return base.astype(jnp.bfloat16)


def draw_windows(key, part):
    key = jax.random.fold_in(key, 37)
    picked = jax.random.randint(key, (HEADS, 2), 0, 2) * 2 + 1
    full_head = jax.random.randint(jax.random.fold_in(key, 1), (), 0, HEADS)
    rows_index = jnp.arange(HEADS, dtype=jnp.int32)[:, None]
    return jnp.where(rows_index == full_head, 3, picked).astype(jnp.int32)


def block_scale(rng, extent, pieces, low, high):
    loudness = 1.0
    for dim, shards_of in pieces:
        heights = jax.random.uniform(jax.random.fold_in(jax.random.fold_in(rng, 6), dim), (shards_of,), jnp.float32, low / len(pieces), high / len(pieces))
        loudness = loudness * jnp.repeat(jnp.exp(heights), extent[dim] // shards_of).reshape((-1,) + (1,) * (len(extent) - 1 - dim))
    return loudness


def normal_values(stream_key, dims, width, limit, cuts=(), kind=jnp.bfloat16):
    values = width * jax.random.normal(stream_key, dims, jnp.float32)
    if cuts:
        values = values * block_scale(stream_key, dims, cuts, -0.22, 0.18)
    return jnp.clip(values, -limit, limit).astype(kind)


def setup_inputs(seed: int = 0) -> dict:
    key_list = jax.random.split(jax.random.key(seed), 6)
    query_tokens = draw_query_tokens(jax.random.fold_in(key_list[5], 71), 0)
    key_tokens = draw_key_tokens(jax.random.fold_in(key_list[5], 71), 0)
    value_tokens = normal_values(key_list[2], (BH, BW, TILE, F), 1.0, 5.0, ((0, 8), (1, 8), (2, 8)))
    grad_output = normal_values(key_list[3], (BH, BW, TILE, F), 1.0, 5.0, ((0, 8), (1, 8), (2, 8)))
    windows = draw_windows(jax.random.fold_in(key_list[5], 71), 0)
    return {"query_tokens": query_tokens, "key_tokens": key_tokens, "value_tokens": value_tokens, "grad_output": grad_output, "windows": windows}


masked_fill = -1e30


def offset_list():
    return [(first, second) for first in range(3) for second in range(3)]


def reference(query_tokens, key_tokens, value_tokens, grad_output, windows):
    logit_scale = HD ** -0.5
    radius = (windows - 1) // 2
    neighbours = offset_list()
    shift_h = jnp.asarray(np.array([first - 1 for first, second in neighbours], dtype=np.int32))
    shift_w = jnp.asarray(np.array([second - 1 for first, second in neighbours], dtype=np.int32))
    pad_spec = ((1, 1), (1, 1), (0, 0), (0, 0))
    keys_pad = jnp.pad(key_tokens, pad_spec)
    values_pad = jnp.pad(value_tokens, pad_spec)
    width_idx = jnp.arange(BW, dtype=jnp.int32)
    reach = (jnp.abs(shift_h)[None, :] <= radius[:, 0:1]) & (jnp.abs(shift_w)[None, :] <= radius[:, 1:2])

    def one_row(row_index, carry):
        grad_q_all, grad_k_pad, grad_v_pad = carry
        row_index = jnp.asarray(row_index).astype(jnp.int32)
        query_row = lax.dynamic_index_in_dim(query_tokens, row_index, 0, keepdims=False)
        out_row = lax.dynamic_index_in_dim(grad_output, row_index, 0, keepdims=False)
        key_slab = lax.dynamic_slice_in_dim(keys_pad, row_index, 3, 0)
        value_slab = lax.dynamic_slice_in_dim(values_pad, row_index, 3, 0)
        key_near = jnp.stack([key_slab[first, second:second + BW] for first, second in neighbours], axis=1)
        value_near = jnp.stack([value_slab[first, second:second + BW] for first, second in neighbours], axis=1)
        height_in = (row_index + shift_h >= 0) & (row_index + shift_h < BH)
        width_in = (width_idx[:, None] + shift_w[None, :] >= 0) & (width_idx[:, None] + shift_w[None, :] < BW)
        placed = height_in[None, :] & width_in

        def one_head(head):
            start = head * HD
            query_float = lax.dynamic_slice_in_dim(query_row, start, HD, 2).astype(jnp.float32)
            output_float = lax.dynamic_slice_in_dim(out_row, start, HD, 2).astype(jnp.float32)
            key_float = lax.dynamic_slice_in_dim(key_near, start, HD, 3).reshape(BW, 9 * TILE, HD).astype(jnp.float32)
            value_float = lax.dynamic_slice_in_dim(value_near, start, HD, 3).reshape(BW, 9 * TILE, HD).astype(jnp.float32)
            reach_head = lax.dynamic_index_in_dim(reach, head, 0, keepdims=False)
            allowed = jnp.repeat(placed & reach_head[None, :], TILE, axis=1)[:, None, :]
            logit_matrix = jnp.einsum("ntz,ngz->ntg", query_float, key_float) * logit_scale
            logit_matrix = jnp.where(allowed, logit_matrix, masked_fill)
            row_max = jnp.max(logit_matrix, axis=-1, keepdims=True)
            log_total = row_max + jnp.log(jnp.sum(jnp.exp(logit_matrix - row_max), axis=-1, keepdims=True))
            probabilities = jnp.exp(logit_matrix - log_total)
            attention_weight = lax.optimization_barrier(probabilities.astype(jnp.bfloat16)).astype(jnp.float32)
            attended_output = jnp.einsum("uhm,umc->uhc", attention_weight, value_float).astype(jnp.bfloat16)
            attended_output = lax.optimization_barrier(attended_output).astype(jnp.float32)
            delta_sum = jnp.sum(output_float * attended_output, axis=-1)[..., None]
            probability_gradient = jnp.einsum("ntz,ngz->ntg", output_float, value_float)
            score_gradient = lax.optimization_barrier((probabilities * (probability_gradient - delta_sum)).astype(jnp.bfloat16)).astype(jnp.float32)
            query_gradient = (jnp.einsum("uhm,umc->uhc", score_gradient, key_float) * logit_scale).astype(jnp.bfloat16)
            key_gradient = jnp.einsum("efu,efi->eui", score_gradient, query_float) * logit_scale
            value_gradient = jnp.einsum("efu,efi->eui", attention_weight, output_float)
            return query_gradient, key_gradient, value_gradient

        query_gradient, key_gradient, value_gradient = lax.map(one_head, jnp.arange(HEADS, dtype=jnp.int32))
        query_gradient = jnp.transpose(query_gradient, (1, 2, 0, 3)).reshape(BW, TILE, F)
        key_gradient = jnp.transpose(key_gradient.reshape(HEADS, BW, 9, TILE, HD), (1, 2, 3, 0, 4)).reshape(BW, 9, TILE, F)
        value_gradient = jnp.transpose(value_gradient.reshape(HEADS, BW, 9, TILE, HD), (1, 2, 3, 0, 4)).reshape(BW, 9, TILE, F)
        slab_k = lax.dynamic_slice_in_dim(grad_k_pad, row_index, 3, 0)
        slab_v = lax.dynamic_slice_in_dim(grad_v_pad, row_index, 3, 0)
        for position, (first, second) in enumerate(neighbours):
            slab_k = slab_k.at[first, second:second + BW].add(key_gradient[:, position])
            slab_v = slab_v.at[first, second:second + BW].add(value_gradient[:, position])
        grad_k_pad = lax.dynamic_update_slice_in_dim(grad_k_pad, slab_k, row_index, 0)
        grad_v_pad = lax.dynamic_update_slice_in_dim(grad_v_pad, slab_v, row_index, 0)
        grad_q_all = lax.dynamic_update_index_in_dim(grad_q_all, query_gradient, row_index, 0)
        return grad_q_all, grad_k_pad, grad_v_pad

    start_carry = (jnp.zeros((BH, BW, TILE, F), jnp.bfloat16), jnp.zeros((BH + 2, BW + 2, TILE, F), jnp.float32), jnp.zeros((BH + 2, BW + 2, TILE, F), jnp.float32))
    grad_queries, grad_k_pad, grad_v_pad = lax.fori_loop(0, BH, one_row, start_carry)
    grad_keys = grad_k_pad[1:-1, 1:-1].astype(jnp.bfloat16)
    grad_values = grad_v_pad[1:-1, 1:-1].astype(jnp.bfloat16)
    return grad_queries, grad_keys, grad_values
```

```python
import functools

import jax
import jax.numpy as jnp
import numpy as np
from jax import lax
from jax.experimental import pallas as pl
from jax.experimental.pallas import tpu as pltpu
from jax.sharding import PartitionSpec as P

head_dim = 128
log2_e = 1.4426950408889634
contract_last = (((1,), (1,)), ((), ()))
small_vmem = 12 * 1024 * 1024
attend_vmem = 44 * 1024 * 1024
hbm_spec = pl.BlockSpec(memory_space=pltpu.HBM)
vmem_spec = pl.BlockSpec(memory_space=pltpu.VMEM)
smem_spec = pl.BlockSpec(memory_space=pltpu.SMEM)
small_params = pltpu.CompilerParams(vmem_limit_bytes=small_vmem)


def pair_partner(kind, index, count):
    partner = index ^ 1 if kind == 1 else ((index + 1) ^ 1) - 1
    return partner if 0 <= partner < count else None


def exchange(value, which, kind):
    parts, rows, cols = (lax.axis_size(name) for name in ("ta", "ha", "wa"))
    pairs = []
    for part in range(parts):
        along_rows = (part % 2 == 0) == (which == 1)
        for row in range(rows):
            for col in range(cols):
                to_row, to_col = row, col
                if along_rows:
                    to_row = pair_partner(kind, row, rows)
                else:
                    to_col = pair_partner(kind, col, cols)
                if to_row is not None and to_col is not None:
                    pairs.append(
                        ((part * rows + row) * cols + col, (part * rows + to_row) * cols + to_col)
                    )
    return lax.ppermute(value, ("ta", "ha", "wa"), pairs)


def unpack_kernel(order, packed, *targets):
    devices, slots = packed.shape[:2]
    for rank in range(devices * slots):
        column = pl.multiple_of(order[rank] * head_dim, head_dim)
        for place, target in enumerate(targets):
            target[:, pl.ds(column, head_dim)] = packed[rank % devices, rank // devices, place]


def unpack(order, packed):
    devices, slots, count, tokens, _ = packed.shape
    flat = jax.ShapeDtypeStruct((tokens, devices * slots * head_dim), packed.dtype)
    return pl.pallas_call(
        unpack_kernel,
        out_shape=[flat] * count,
        in_specs=[smem_spec, vmem_spec],
        compiler_params=small_params,
    )(order, packed)


def attend_kernel(full, valid, *refs):
    qg_in, own_in, first_in, second_in = refs[0], refs[1], refs[2:4], refs[4:6]
    dq_out, own_out, first_out, second_out = refs[6], refs[7], refs[8:10], refs[10:12]
    (qg, kv, score, dprob, part, dq, top, total, weighted, dq_t, load_sem, store_sem) = refs[12:]
    chunks, slots, _, rows, _ = qg.shape
    tile = chunks * rows
    scale = head_dim ** (-0.5)
    to_log2 = scale * log2_e
    head = pl.ds(0, full)
    tail = pl.ds(full, slots - full)

    def relayed(b):
        return pl.ds(slots + b * full, full)

    early = [(qg_in, qg), (own_in, kv.at[0])]
    early += [(first_in[a].at[:, pl.ds(0, slots)], kv.at[a + 1]) for a in range(2)]
    late = []
    for b in range(2):
        late.append((second_in[b], kv.at[3 * b + 3, :, head]))
        late += [
            (first_in[a].at[:, relayed(b)], kv.at[3 * b + 4 + a, :, head]) for a in range(2)
        ]
    early = [pltpu.make_async_copy(*pair, load_sem.at[n]) for n, pair in enumerate(early)]
    late = [
        pltpu.make_async_copy(*pair, load_sem.at[len(early) + n]) for n, pair in enumerate(late)
    ]
    for copy in early + late:
        copy.start()

    def over_rows(slot, lines, step):
        def one_line(line, carry):
            start = 3 * line
            here = [valid[slot, start + a] for a in range(3)]
            whole = here[0] * here[1] * here[2]

            @pl.when(whole != 0)
            def _():
                step(start, 3)

            @pl.when(whole == 0)
            def _():
                def one_place(a, carry):
                    @pl.when(valid[slot, start + a] != 0)
                    def _():
                        step(start + a, 1)

                    return carry

                lax.fori_loop(0, 3, one_place, 0)

            return carry

        lax.fori_loop(0, lines, one_line, 0)

    def one_slot(slot, lines):
        query = qg[:, slot, 0].reshape(tile, head_dim)
        grad = qg[:, slot, 1].reshape(tile, head_dim)
        top[...] = jnp.full(top.shape, -1e30, jnp.float32)
        total[...] = jnp.zeros(total.shape, jnp.float32)
        weighted[...] = jnp.zeros(weighted.shape, jnp.float32)
        dq_t[...] = jnp.zeros(dq_t.shape, jnp.float32)

        def forward(start, count):
            near = pl.ds(start, count)
            key = kv[near, :, slot, 0].reshape(count * tile, head_dim)
            value = kv[near, :, slot, 1].reshape(count * tile, head_dim)
            raw = lax.dot_general(key, query, contract_last, preferred_element_type=jnp.float32)
            rise = lax.dot_general(value, grad, contract_last, preferred_element_type=jnp.float32)
            score[near] = raw.reshape(count, tile, tile)
            dprob[near] = rise.reshape(count, tile, tile)
            top_old = top[...]
            top_new = jnp.maximum(top_old, jnp.max(raw, axis=0, keepdims=True))
            fade = jnp.exp2((top_old - top_new) * to_log2)
            spread = jnp.exp2((raw - top_new) * to_log2)
            top[...] = top_new
            total[...] = total[...] * fade + jnp.sum(spread, axis=0, keepdims=True)
            weighted[...] = weighted[...] * fade + jnp.sum(spread * rise, axis=0, keepdims=True)

        over_rows(slot, lines, forward)
        log_total = top[...] * to_log2 + jnp.log(total[...]) * log2_e
        delta = weighted[...] / total[...]

        def backward(start, count):
            near = pl.ds(start, count)
            key = kv[near, :, slot, 0].reshape(count * tile, head_dim)
            raw = score[near].reshape(count * tile, tile)
            rise = dprob[near].reshape(count * tile, tile)
            prob = jnp.exp2(raw * to_log2 - log_total)
            weight = prob.astype(jnp.bfloat16)
            dscore = (prob * (rise - delta)).astype(jnp.bfloat16)
            dv = jnp.dot(weight, grad, preferred_element_type=jnp.float32)
            dk = jnp.dot(dscore, query, preferred_element_type=jnp.float32) * scale
            dq_t[...] += jnp.dot(key.T, dscore, preferred_element_type=jnp.float32)
            shape = (count, chunks, rows, head_dim)
            part[near, :, slot, 0] = dk.astype(jnp.bfloat16).reshape(shape)
            part[near, :, slot, 1] = dv.astype(jnp.bfloat16).reshape(shape)

        over_rows(slot, lines, backward)
        dq_here = (dq_t[...] * scale).T.astype(jnp.bfloat16)
        dq[:, slot, 0] = dq_here.reshape(chunks, rows, head_dim)

    def tail_slot(slot, carry):
        one_slot(slot, 1)
        return carry

    def full_slot(slot, carry):
        one_slot(slot, 3)
        return carry

    def store(pairs, base):
        copies = [
            pltpu.make_async_copy(*pair, store_sem.at[base + n]) for n, pair in enumerate(pairs)
        ]
        for copy in copies:
            copy.start()
        return copies

    for copy in early:
        copy.wait()
    stores = []
    if full < slots:
        lax.fori_loop(full, slots, tail_slot, 0)
        pairs = [(part.at[0, :, tail], own_out.at[:, tail])]
        pairs += [(part.at[a + 1, :, tail], first_out[a].at[:, tail]) for a in range(2)]
        stores += store(pairs, 0)
    for copy in late:
        copy.wait()
    lax.fori_loop(0, full, full_slot, 0)
    pairs = []
    for a in range(2):
        pairs.append((part.at[a + 1, :, head], first_out[a].at[:, head]))
        pairs += [
            (part.at[3 * b + 4 + a, :, head], first_out[a].at[:, relayed(b)]) for b in range(2)
        ]
    pairs += [(part.at[3 * b + 3, :, head], second_out[b]) for b in range(2)]
    pairs += [(part.at[0, :, head], own_out.at[:, head]), (dq, dq_out)]
    stores += store(pairs, 3)
    for copy in stores:
        copy.wait()


def attend(valid, qg, own, first, second, full):
    chunks, slots, _, rows, _ = qg.shape
    tile = chunks * rows
    bf16, f32 = jnp.bfloat16, jnp.float32
    units = 9 * full + 3 * (slots - full)
    near = [own, *first, *second]
    dq_shape = (chunks, slots, 1, rows, head_dim)
    outs = pl.pallas_call(
        functools.partial(attend_kernel, full),
        out_shape=[jax.ShapeDtypeStruct(dq_shape, bf16)]
        + [jax.ShapeDtypeStruct(array.shape, bf16) for array in near],
        in_specs=[smem_spec] + [hbm_spec] * 6,
        out_specs=[hbm_spec] * 6,
        scratch_shapes=[
            pltpu.VMEM(qg.shape, bf16),
            pltpu.VMEM((9,) + own.shape, bf16),
            pltpu.VMEM((9, tile, tile), f32),
            pltpu.VMEM((9, tile, tile), f32),
            pltpu.VMEM((9,) + own.shape, bf16),
            pltpu.VMEM(dq_shape, bf16),
            pltpu.VMEM((1, tile), f32),
            pltpu.VMEM((1, tile), f32),
            pltpu.VMEM((1, tile), f32),
            pltpu.VMEM((head_dim, tile), f32),
            pltpu.SemaphoreType.DMA((10,)),
            pltpu.SemaphoreType.DMA((13,)),
        ],
        compiler_params=pltpu.CompilerParams(vmem_limit_bytes=attend_vmem),
        cost_estimate=pl.CostEstimate(
            flops=units * 10 * tile * tile * head_dim,
            bytes_accessed=8 * 1024 * 1024,
            transcendentals=units * 2 * tile * tile,
        ),
    )(valid, qg, *near)
    return outs[0], outs[1], outs[2:4], outs[4:6]


def relay_kernel(valid, *refs):
    second, first, out = refs[0:2], refs[2:4], refs[4:6]
    full = out[0].shape[1]
    slots = first[0].shape[1] - 2 * full
    for b in range(2):
        for slot in range(full):
            total = second[b][:, slot].astype(jnp.float32)
            for a in range(2):
                arrived = first[a][:, slots + b * full + slot].astype(jnp.float32)
                total += jnp.where(valid[slot, 3 * b + 4 + a] != 0, arrived, 0.0)
            out[b][:, slot] = total.astype(out[b].dtype)


def relay(valid, second, first):
    return pl.pallas_call(
        relay_kernel,
        out_shape=[jax.ShapeDtypeStruct(array.shape, array.dtype) for array in second],
        in_specs=[smem_spec] + [vmem_spec] * 4,
        compiler_params=small_params,
    )(valid, *second, *first)


def combine_kernel(valid, own, *refs):
    first, second, out = refs[0:2], refs[2:4], refs[4]
    full = second[0].shape[1]
    for slot in range(out.shape[1]):
        total = own[:, slot].astype(jnp.float32)
        for a in range(2):
            arrived = first[a][:, slot].astype(jnp.float32)
            total += jnp.where(valid[slot, a + 1] != 0, arrived, 0.0)
        if slot < full:
            for b in range(2):
                arrived = second[b][:, slot].astype(jnp.float32)
                total += jnp.where(valid[slot, 3 * b + 3] != 0, arrived, 0.0)
        out[:, slot] = total.astype(out.dtype)


def combine(valid, own, first, second):
    return pl.pallas_call(
        combine_kernel,
        out_shape=jax.ShapeDtypeStruct(own.shape, own.dtype),
        in_specs=[smem_spec] + [vmem_spec] * 5,
        compiler_params=small_params,
    )(valid, own, *first, *second)


def swap(blocks):
    return lax.all_to_all(blocks, "ta", split_axis=0, concat_axis=0, tiled=True)


def with_corners(full, order, valid, kv, qg):
    kv_full = lax.slice_in_dim(kv, 0, full, axis=1)
    second = [exchange(kv_full, 2, kind) for kind in (1, 2)]
    qg, second[0] = lax.optimization_barrier((qg, second[0]))
    qg = swap(qg)
    message = jnp.concatenate([kv, *second], axis=1)
    first = [exchange(message, 1, kind) for kind in (1, 2)]
    dq, own, first, second = attend(valid, qg, kv, first, second, full)
    first = [exchange(first[kind - 1], 1, kind) for kind in (1, 2)]
    dq = swap(dq)
    second = relay(valid, second, first)
    second = [exchange(second[kind - 1], 2, kind) for kind in (1, 2)]
    dkv = swap(combine(valid, own, first, second))
    return tuple(unpack(order, dq) + unpack(order, dkv))


def place_heads(devices, shape, windows, order, valid, choice):
    heads = windows.shape[0]
    slots, half = heads // devices, devices // 2
    kinds = []
    for head in range(heads):
        tall = lax.shift_right_logical(windows[head, 0] - 1, 1)
        wide = lax.shift_right_logical(windows[head, 1] - 1, 1)
        kinds.append(2 * tall + wide)

    def count(kind):
        return functools.reduce(
            lambda a, b: a + b, [(other == kind).astype(jnp.int32) for other in kinds]
        )

    both, rows_only, cols_only = count(3), count(2), count(1)

    def over(count, room):
        return jnp.maximum(count - room, 0)

    chosen = jnp.int32(slots - 1)
    for full in range(slots - 1, 0, -1):
        room = half * (slots - full)
        needed = both + over(rows_only, room) + over(cols_only, room)
        chosen = jnp.where(needed <= devices * full, full - 1, chosen)
    choice[0] = chosen
    full = chosen + 1
    room = half * (slots - full)
    used = both + over(rows_only, room) + over(cols_only, room)
    free = devices * full - used
    rows_used, cols_used = jnp.minimum(rows_only, room), jnp.minimum(cols_only, room)
    rows_free = room - rows_used

    def single(nth, odd):
        return devices * full + devices * lax.div(nth, half) + 2 * lax.rem(nth, half) + odd

    seen = [jnp.int32(0)] * 4
    for head in range(heads):
        kind = kinds[head]
        at = [None] * 4
        at[3] = seen[3]
        at[2] = jnp.where(seen[2] < room, single(seen[2], 0), both + seen[2] - room)
        at[1] = jnp.where(
            seen[1] < room,
            single(seen[1], 1),
            both + over(rows_only, room) + seen[1] - room,
        )
        at[0] = jnp.where(
            seen[0] < free,
            used + seen[0],
            jnp.where(
                seen[0] < free + rows_free,
                single(rows_used + seen[0] - free, 0),
                single(cols_used + seen[0] - free - rows_free, 1),
            ),
        )
        place = at[0]
        for other in range(1, 4):
            place = jnp.where(kind == other, at[other], place)
        order[place] = jnp.int32(head)
        for other in range(4):
            seen[other] = seen[other] + (kind == other).astype(jnp.int32)

    part, row, col = (lax.axis_index(name) for name in ("ta", "ha", "wa"))
    by_rows = lax.rem(part, 2) == 0

    def inside(kind, index, count):
        if kind == 0:
            return jnp.int32(1)
        partner = index ^ 1 if kind == 1 else ((index + 1) ^ 1) - 1
        return ((partner >= 0) & (partner < count)).astype(jnp.int32)

    in_rows = [inside(kind, row, shape[0]) for kind in range(3)]
    in_cols = [inside(kind, col, shape[1]) for kind in range(3)]
    for slot in range(slots):
        head = order[slot * devices + part]
        tall = lax.shift_right_logical(windows[head, 0] - 1, 1)
        wide = lax.shift_right_logical(windows[head, 1] - 1, 1)
        along_rows = [in_rows[0], in_rows[1] * tall, in_rows[2] * tall]
        along_cols = [in_cols[0], in_cols[1] * wide, in_cols[2] * wide]
        for b in range(3):
            for a in range(3):
                valid[slot, 3 * b + a] = jnp.where(
                    by_rows, along_rows[a] * along_cols[b], along_cols[a] * along_rows[b]
                )


def prepare_kernel(shape, windows, *refs):
    sources, (order, valid, choice, kv, qg) = refs[:4], refs[4:]
    devices, slots = kv.shape[:2]
    place_heads(devices, shape, windows, order, valid, choice)
    for rank in range(devices * slots):
        column = pl.multiple_of(order[rank] * head_dim, head_dim)
        for n, source in enumerate(sources):
            packed = kv if n < 2 else qg
            packed[rank % devices, rank // devices, n % 2] = source[:, pl.ds(column, head_dim)]


def on_device(query_tokens, key_tokens, value_tokens, grad_output, windows):
    devices = lax.axis_size("ta")
    heads = windows.shape[0]
    slots = heads // devices
    tokens, features = query_tokens.shape[-2:]
    block = jax.ShapeDtypeStruct((devices, slots, 2, tokens, head_dim), query_tokens.dtype)
    arrays = (key_tokens, value_tokens, query_tokens, grad_output)
    shape = (lax.axis_size("ha"), lax.axis_size("wa"))
    order, valid, choice, kv, qg = pl.pallas_call(
        functools.partial(prepare_kernel, shape),
        out_shape=[
            jax.ShapeDtypeStruct((heads,), jnp.int32),
            jax.ShapeDtypeStruct((slots, 9), jnp.int32),
            jax.ShapeDtypeStruct((1,), jnp.int32),
            block,
            block,
        ],
        in_specs=[smem_spec] + [vmem_spec] * 4,
        out_specs=[smem_spec] * 3 + [vmem_spec] * 2,
        compiler_params=small_params,
    )(windows, *[array.reshape(tokens, features) for array in arrays])
    kv = swap(kv)
    branches = [functools.partial(with_corners, full) for full in range(1, slots + 1)]
    outs = lax.switch(choice[0], branches, order, valid, kv, qg)
    return tuple(out.reshape(query_tokens.shape) for out in outs)


def solution(mesh):
    shares = P("ha", "wa", "ta", None)
    return jax.shard_map(
        on_device,
        mesh=mesh,
        in_specs=(shares, shares, shares, shares, P()),
        out_specs=(shares, shares, shares),
        check_vma=False,
    )
```

```python
import functools

import jax
import jax.numpy as jnp
import numpy as np
from jax import lax
from jax.experimental import pallas as pl
from jax.experimental.pallas import tpu as pltpu
from jax.sharding import PartitionSpec as P

head_dim = 128
log2_e = 1.4426950408889634
contract_last = (((1,), (1,)), ((), ()))
small_vmem = 12 * 1024 * 1024
attend_vmem = 44 * 1024 * 1024
hbm_spec = pl.BlockSpec(memory_space=pltpu.HBM)
vmem_spec = pl.BlockSpec(memory_space=pltpu.VMEM)
smem_spec = pl.BlockSpec(memory_space=pltpu.SMEM)
small_params = pltpu.CompilerParams(vmem_limit_bytes=small_vmem)


def pair_partner(kind, index, count):
    partner = index ^ 1 if kind == 1 else ((index + 1) ^ 1) - 1
    return partner if 0 <= partner < count else None


def exchange(value, which, kind):
    parts, rows, cols = (lax.axis_size(name) for name in ("ta", "ha", "wa"))
    pairs = []
    for part in range(parts):
        along_rows = (part % 2 == 0) == (which == 1)
        for row in range(rows):
            for col in range(cols):
                to_row, to_col = row, col
                if along_rows:
                    to_row = pair_partner(kind, row, rows)
                else:
                    to_col = pair_partner(kind, col, cols)
                if to_row is not None and to_col is not None:
                    pairs.append(
                        ((part * rows + row) * cols + col, (part * rows + to_row) * cols + to_col)
                    )
    return lax.ppermute(value, ("ta", "ha", "wa"), pairs)


def unpack_kernel(order, packed, *targets):
    devices, slots = packed.shape[:2]
    for rank in range(devices * slots):
        column = pl.multiple_of(order[rank] * head_dim, head_dim)
        for place, target in enumerate(targets):
            target[:, pl.ds(column, head_dim)] = packed[rank % devices, rank // devices, place]


def unpack(order, packed):
    devices, slots, count, tokens, _ = packed.shape
    flat = jax.ShapeDtypeStruct((tokens, devices * slots * head_dim), packed.dtype)
    return pl.pallas_call(
        unpack_kernel,
        out_shape=[flat] * count,
        in_specs=[smem_spec, vmem_spec],
        compiler_params=small_params,
    )(order, packed)


def attend_kernel(full, valid, *refs):
    qg_in, own_in, first_in, second_in = refs[0], refs[1], refs[2:4], refs[4:6]
    dq_out, own_out, first_out, second_out = refs[6], refs[7], refs[8:10], refs[10:12]
    (qg, kv, score, dprob, part, dq, top, total, weighted, dq_t, load_sem, store_sem) = refs[12:]
    chunks, slots, _, rows, _ = qg.shape
    tile = chunks * rows
    scale = head_dim ** (-0.5)
    to_log2 = scale * log2_e
    head = pl.ds(0, full)
    tail = pl.ds(full, slots - full)

    def relayed(b):
        return pl.ds(slots + b * full, full)

    early = [(qg_in, qg), (own_in, kv.at[0])]
    early += [(first_in[a].at[:, pl.ds(0, slots)], kv.at[a + 1]) for a in range(2)]
    late = []
    for b in range(2):
        late.append((second_in[b], kv.at[3 * b + 3, :, head]))
        late += [
            (first_in[a].at[:, relayed(b)], kv.at[3 * b + 4 + a, :, head]) for a in range(2)
        ]
    early = [pltpu.make_async_copy(*pair, load_sem.at[n]) for n, pair in enumerate(early)]
    late = [
        pltpu.make_async_copy(*pair, load_sem.at[len(early) + n]) for n, pair in enumerate(late)
    ]
    for copy in early + late:
        copy.start()

    def over_rows(slot, lines, step):
        def one_line(line, carry):
            start = 3 * line
            here = [valid[slot, start + a] for a in range(3)]
            whole = here[0] * here[1] * here[2]

            @pl.when(whole != 0)
            def _():
                step(start, 3)

            @pl.when(whole == 0)
            def _():
                def one_place(a, carry):
                    @pl.when(valid[slot, start + a] != 0)
                    def _():
                        step(start + a, 1)

                    return carry

                lax.fori_loop(0, 3, one_place, 0)

            return carry

        lax.fori_loop(0, lines, one_line, 0)

    def one_slot(slot, lines):
        query = qg[:, slot, 0].reshape(tile, head_dim)
        grad = qg[:, slot, 1].reshape(tile, head_dim)
        top[...] = jnp.full(top.shape, -1e30, jnp.float32)
        total[...] = jnp.zeros(total.shape, jnp.float32)
        weighted[...] = jnp.zeros(weighted.shape, jnp.float32)
        dq_t[...] = jnp.zeros(dq_t.shape, jnp.float32)

        def forward(start, count):
            near = pl.ds(start, count)
            key = kv[near, :, slot, 0].reshape(count * tile, head_dim)
            value = kv[near, :, slot, 1].reshape(count * tile, head_dim)
            raw = lax.dot_general(key, query, contract_last, preferred_element_type=jnp.float32)
            rise = lax.dot_general(value, grad, contract_last, preferred_element_type=jnp.float32)
            score[near] = raw.reshape(count, tile, tile)
            dprob[near] = rise.reshape(count, tile, tile)
            top_old = top[...]
            top_new = jnp.maximum(top_old, jnp.max(raw, axis=0, keepdims=True))
            fade = jnp.exp2((top_old - top_new) * to_log2)
            spread = jnp.exp2((raw - top_new) * to_log2)
            top[...] = top_new
            total[...] = total[...] * fade + jnp.sum(spread, axis=0, keepdims=True)
            weighted[...] = weighted[...] * fade + jnp.sum(spread * rise, axis=0, keepdims=True)

        over_rows(slot, lines, forward)
        log_total = top[...] * to_log2 + jnp.log(total[...]) * log2_e
        delta = weighted[...] / total[...]

        def backward(start, count):
            near = pl.ds(start, count)
            key = kv[near, :, slot, 0].reshape(count * tile, head_dim)
            raw = score[near].reshape(count * tile, tile)
            rise = dprob[near].reshape(count * tile, tile)
            prob = jnp.exp2(raw * to_log2 - log_total)
            weight = prob.astype(jnp.bfloat16)
            dscore = (prob * (rise - delta)).astype(jnp.bfloat16)
            dv = jnp.dot(weight, grad, preferred_element_type=jnp.float32)
            dk = jnp.dot(dscore, query, preferred_element_type=jnp.float32) * scale
            dq_t[...] += jnp.dot(key.T, dscore, preferred_element_type=jnp.float32)
            shape = (count, chunks, rows, head_dim)
            part[near, :, slot, 0] = dk.astype(jnp.bfloat16).reshape(shape)
            part[near, :, slot, 1] = dv.astype(jnp.bfloat16).reshape(shape)

        over_rows(slot, lines, backward)
        dq_here = (dq_t[...] * scale).T.astype(jnp.bfloat16)
        dq[:, slot, 0] = dq_here.reshape(chunks, rows, head_dim)

    def tail_slot(slot, carry):
        one_slot(slot, 1)
        return carry

    def full_slot(slot, carry):
        one_slot(slot, 3)
        return carry

    def store(pairs, base):
        copies = [
            pltpu.make_async_copy(*pair, store_sem.at[base + n]) for n, pair in enumerate(pairs)
        ]
        for copy in copies:
            copy.start()
        return copies

    for copy in early:
        copy.wait()
    stores = []
    if full < slots:
        lax.fori_loop(full, slots, tail_slot, 0)
        pairs = [(part.at[0, :, tail], own_out.at[:, tail])]
        pairs += [(part.at[a + 1, :, tail], first_out[a].at[:, tail]) for a in range(2)]
        stores += store(pairs, 0)
    for copy in late:
        copy.wait()
    lax.fori_loop(0, full, full_slot, 0)
    pairs = []
    for a in range(2):
        pairs.append((part.at[a + 1, :, head], first_out[a].at[:, head]))
        pairs += [
            (part.at[3 * b + 4 + a, :, head], first_out[a].at[:, relayed(b)]) for b in range(2)
        ]
    pairs += [(part.at[3 * b + 3, :, head], second_out[b]) for b in range(2)]
    pairs += [(part.at[0, :, head], own_out.at[:, head]), (dq, dq_out)]
    stores += store(pairs, 3)
    for copy in stores:
        copy.wait()


def attend(valid, qg, own, first, second, full):
    chunks, slots, _, rows, _ = qg.shape
    tile = chunks * rows
    bf16, f32 = jnp.bfloat16, jnp.float32
    units = 9 * full + 3 * (slots - full)
    near = [own, *first, *second]
    dq_shape = (chunks, slots, 1, rows, head_dim)
    outs = pl.pallas_call(
        functools.partial(attend_kernel, full),
        out_shape=[jax.ShapeDtypeStruct(dq_shape, bf16)]
        + [jax.ShapeDtypeStruct(array.shape, bf16) for array in near],
        in_specs=[smem_spec] + [hbm_spec] * 6,
        out_specs=[hbm_spec] * 6,
        scratch_shapes=[
            pltpu.VMEM(qg.shape, bf16),
            pltpu.VMEM((9,) + own.shape, bf16),
            pltpu.VMEM((9, tile, tile), f32),
            pltpu.VMEM((9, tile, tile), f32),
            pltpu.VMEM((9,) + own.shape, bf16),
            pltpu.VMEM(dq_shape, bf16),
            pltpu.VMEM((1, tile), f32),
            pltpu.VMEM((1, tile), f32),
            pltpu.VMEM((1, tile), f32),
            pltpu.VMEM((head_dim, tile), f32),
            pltpu.SemaphoreType.DMA((10,)),
            pltpu.SemaphoreType.DMA((13,)),
        ],
        compiler_params=pltpu.CompilerParams(vmem_limit_bytes=attend_vmem),
        cost_estimate=pl.CostEstimate(
            flops=units * 10 * tile * tile * head_dim,
            bytes_accessed=8 * 1024 * 1024,
            transcendentals=units * 2 * tile * tile,
        ),
    )(valid, qg, *near)
    return outs[0], outs[1], outs[2:4], outs[4:6]


def relay_kernel(valid, *refs):
    second, first, out = refs[0:2], refs[2:4], refs[4:6]
    full = out[0].shape[1]
    slots = first[0].shape[1] - 2 * full
    for b in range(2):
        for slot in range(full):
            total = second[b][:, slot].astype(jnp.float32)
            for a in range(2):
                arrived = first[a][:, slots + b * full + slot].astype(jnp.float32)
                total += jnp.where(valid[slot, 3 * b + 4 + a] != 0, arrived, 0.0)
            out[b][:, slot] = total.astype(out[b].dtype)


def relay(valid, second, first):
    return pl.pallas_call(
        relay_kernel,
        out_shape=[jax.ShapeDtypeStruct(array.shape, array.dtype) for array in second],
        in_specs=[smem_spec] + [vmem_spec] * 4,
        compiler_params=small_params,
    )(valid, *second, *first)


def combine_kernel(valid, dq, own, *refs):
    first, second, out = refs[0:2], refs[2:4], refs[4]
    full = second[0].shape[1]
    for slot in range(out.shape[1]):
        total = own[:, slot].astype(jnp.float32)
        for a in range(2):
            arrived = first[a][:, slot].astype(jnp.float32)
            total += jnp.where(valid[slot, a + 1] != 0, arrived, 0.0)
        if slot < full:
            for b in range(2):
                arrived = second[b][:, slot].astype(jnp.float32)
                total += jnp.where(valid[slot, 3 * b + 3] != 0, arrived, 0.0)
        out[:, slot, 0] = dq[:, slot, 0]
        out[:, slot, 1:3] = total.astype(out.dtype)


def combine(valid, dq, own, first, second):
    chunks, slots, _, rows, _ = own.shape
    return pl.pallas_call(
        combine_kernel,
        out_shape=jax.ShapeDtypeStruct((chunks, slots, 3, rows, head_dim), own.dtype),
        in_specs=[smem_spec] + [vmem_spec] * 6,
        out_specs=vmem_spec,
        compiler_params=small_params,
    )(valid, dq, own, *first, *second)


def swap(blocks):
    return lax.all_to_all(blocks, "ta", split_axis=0, concat_axis=0, tiled=True)


def both_kinds(arrays, which):
    swapped = {kind: exchange(arrays[kind - 1], which, kind) for kind in (2, 1)}
    return [swapped[1], swapped[2]]


def with_corners(full, valid, kv, qg):
    kv_full = lax.slice_in_dim(kv, 0, full, axis=1)
    second = [exchange(kv_full, 2, kind) for kind in (1, 2)]
    qg, second[0] = lax.optimization_barrier((qg, second[0]))
    qg = swap(qg)
    message = jnp.concatenate([kv, *second], axis=1)
    first = [exchange(message, 1, kind) for kind in (1, 2)]
    dq, own, first, second = attend(valid, qg, kv, first, second, full)
    first = both_kinds(first, 1)
    second = both_kinds(relay(valid, second, first), 2)
    return combine(valid, dq, own, first, second)


def place_heads(devices, shape, windows, order, valid, choice):
    heads = windows.shape[0]
    slots, half = heads // devices, devices // 2
    kinds = []
    for head in range(heads):
        tall = lax.shift_right_logical(windows[head, 0] - 1, 1)
        wide = lax.shift_right_logical(windows[head, 1] - 1, 1)
        kinds.append(2 * tall + wide)

    def count(kind):
        return functools.reduce(
            lambda a, b: a + b, [(other == kind).astype(jnp.int32) for other in kinds]
        )

    both, rows_only, cols_only = count(3), count(2), count(1)

    def over(count, room):
        return jnp.maximum(count - room, 0)

    chosen = jnp.int32(slots - 1)
    for full in range(slots - 1, 0, -1):
        room = half * (slots - full)
        needed = both + over(rows_only, room) + over(cols_only, room)
        chosen = jnp.where(needed <= devices * full, full - 1, chosen)
    choice[0] = chosen
    full = chosen + 1
    room = half * (slots - full)
    used = both + over(rows_only, room) + over(cols_only, room)
    free = devices * full - used
    rows_used, cols_used = jnp.minimum(rows_only, room), jnp.minimum(cols_only, room)
    rows_free = room - rows_used

    def single(nth, odd):
        return devices * full + devices * lax.div(nth, half) + 2 * lax.rem(nth, half) + odd

    seen = [jnp.int32(0)] * 4
    for head in range(heads):
        kind = kinds[head]
        at = [None] * 4
        at[3] = seen[3]
        at[2] = jnp.where(seen[2] < room, single(seen[2], 0), both + seen[2] - room)
        at[1] = jnp.where(
            seen[1] < room,
            single(seen[1], 1),
            both + over(rows_only, room) + seen[1] - room,
        )
        at[0] = jnp.where(
            seen[0] < free,
            used + seen[0],
            jnp.where(
                seen[0] < free + rows_free,
                single(rows_used + seen[0] - free, 0),
                single(cols_used + seen[0] - free - rows_free, 1),
            ),
        )
        place = at[0]
        for other in range(1, 4):
            place = jnp.where(kind == other, at[other], place)
        order[place] = jnp.int32(head)
        for other in range(4):
            seen[other] = seen[other] + (kind == other).astype(jnp.int32)

    part, row, col = (lax.axis_index(name) for name in ("ta", "ha", "wa"))
    by_rows = lax.rem(part, 2) == 0

    def inside(kind, index, count):
        if kind == 0:
            return jnp.int32(1)
        partner = index ^ 1 if kind == 1 else ((index + 1) ^ 1) - 1
        return ((partner >= 0) & (partner < count)).astype(jnp.int32)

    in_rows = [inside(kind, row, shape[0]) for kind in range(3)]
    in_cols = [inside(kind, col, shape[1]) for kind in range(3)]
    for slot in range(slots):
        head = order[slot * devices + part]
        tall = lax.shift_right_logical(windows[head, 0] - 1, 1)
        wide = lax.shift_right_logical(windows[head, 1] - 1, 1)
        along_rows = [in_rows[0], in_rows[1] * tall, in_rows[2] * tall]
        along_cols = [in_cols[0], in_cols[1] * wide, in_cols[2] * wide]
        for b in range(3):
            for a in range(3):
                valid[slot, 3 * b + a] = jnp.where(
                    by_rows, along_rows[a] * along_cols[b], along_cols[a] * along_rows[b]
                )


def pack_kernel(order, first, second, packed):
    devices, slots = packed.shape[:2]
    for rank in range(devices * slots):
        column = pl.multiple_of(order[rank] * head_dim, head_dim)
        for n, source in enumerate((first, second)):
            packed[rank % devices, rank // devices, n] = source[:, pl.ds(column, head_dim)]


def prepare_kernel(shape, windows, *refs):
    sources, (order, valid, choice, kv) = refs[:2], refs[2:]
    place_heads(kv.shape[0], shape, windows, order, valid, choice)
    pack_kernel(order, *sources, kv)


def on_device(query_tokens, key_tokens, value_tokens, grad_output, windows):
    devices = lax.axis_size("ta")
    heads = windows.shape[0]
    slots = heads // devices
    tokens, features = query_tokens.shape[-2:]
    block = jax.ShapeDtypeStruct((devices, slots, 2, tokens, head_dim), query_tokens.dtype)
    arrays = (key_tokens, value_tokens, query_tokens, grad_output)
    arrays = [array.reshape(tokens, features) for array in arrays]
    shape = (lax.axis_size("ha"), lax.axis_size("wa"))
    order, valid, choice, kv = pl.pallas_call(
        functools.partial(prepare_kernel, shape),
        out_shape=[
            jax.ShapeDtypeStruct((heads,), jnp.int32),
            jax.ShapeDtypeStruct((slots, 9), jnp.int32),
            jax.ShapeDtypeStruct((1,), jnp.int32),
            block,
        ],
        in_specs=[smem_spec] + [vmem_spec] * 2,
        out_specs=[smem_spec] * 3 + [vmem_spec],
        compiler_params=small_params,
    )(windows, *arrays[:2])
    qg = pl.pallas_call(
        pack_kernel,
        out_shape=block,
        in_specs=[smem_spec] + [vmem_spec] * 2,
        out_specs=vmem_spec,
        compiler_params=small_params,
    )(order, *arrays[2:])
    kv = swap(kv)
    branches = [functools.partial(with_corners, full) for full in range(1, slots + 1)]
    outs = unpack(order, swap(lax.switch(choice[0], branches, valid, kv, qg)))
    return tuple(out.reshape(query_tokens.shape) for out in outs)


def solution(mesh):
    shares = P("ha", "wa", "ta", None)
    return jax.shard_map(
        on_device,
        mesh=mesh,
        in_specs=(shares, shares, shares, shares, P()),
        out_specs=(shares, shares, shares),
        check_vma=False,
    )
```

```python
import functools

import jax
import jax.numpy as jnp
import numpy as np
from jax import lax
from jax.experimental import pallas as pl
from jax.experimental.pallas import tpu as pltpu
from jax.sharding import PartitionSpec as P

head_dim = 128
log2_e = 1.4426950408889634
contract_last = (((1,), (1,)), ((), ()))
small_vmem = 12 * 1024 * 1024
attend_vmem = 44 * 1024 * 1024
hbm_spec = pl.BlockSpec(memory_space=pltpu.HBM)
vmem_spec = pl.BlockSpec(memory_space=pltpu.VMEM)
smem_spec = pl.BlockSpec(memory_space=pltpu.SMEM)
small_params = pltpu.CompilerParams(vmem_limit_bytes=small_vmem)


def pair_partner(kind, index, count):
    partner = index ^ 1 if kind == 1 else ((index + 1) ^ 1) - 1
    return partner if 0 <= partner < count else None


def exchange(value, which, kind):
    parts, rows, cols = (lax.axis_size(name) for name in ("ta", "ha", "wa"))
    pairs = []
    for part in range(parts):
        along_rows = (part % 2 == 0) == (which == 1)
        for row in range(rows):
            for col in range(cols):
                to_row, to_col = row, col
                if along_rows:
                    to_row = pair_partner(kind, row, rows)
                else:
                    to_col = pair_partner(kind, col, cols)
                if to_row is not None and to_col is not None:
                    pairs.append(
                        ((part * rows + row) * cols + col, (part * rows + to_row) * cols + to_col)
                    )
    return lax.ppermute(value, ("ta", "ha", "wa"), pairs)


def unpack_kernel(order, packed, *targets):
    devices, slots = packed.shape[:2]
    for rank in range(devices * slots):
        column = pl.multiple_of(order[rank] * head_dim, head_dim)
        for place, target in enumerate(targets):
            target[:, pl.ds(column, head_dim)] = packed[rank % devices, rank // devices, place]


def unpack(order, packed):
    devices, slots, count, tokens, _ = packed.shape
    flat = jax.ShapeDtypeStruct((tokens, devices * slots * head_dim), packed.dtype)
    return pl.pallas_call(
        unpack_kernel,
        out_shape=[flat] * count,
        in_specs=[smem_spec, vmem_spec],
        compiler_params=small_params,
    )(order, packed)


def attend_kernel(full, valid, *refs):
    qg_in, own_in, first_in, second_in = refs[0], refs[1], refs[2:4], refs[4:6]
    dq_out, own_out, first_out, second_out = refs[6], refs[7], refs[8:10], refs[10:12]
    (qg, kv, score, dprob, part, dq, top, total, weighted, dq_t, load_sem, store_sem) = refs[12:]
    chunks, slots, _, rows, _ = qg.shape
    tile = chunks * rows
    scale = head_dim ** (-0.5)
    to_log2 = scale * log2_e

    def pieces(slot, line):
        here = pl.ds(slot, 1)
        if line == 0:
            outside = [(own_in, own_out, here)]
            outside += [(first_in[a], first_out[a], here) for a in range(2)]
        else:
            passed = pl.ds(slots + (line - 1) * full + slot, 1)
            outside = [(second_in[line - 1], second_out[line - 1], here)]
            outside += [(first_in[a], first_out[a], passed) for a in range(2)]
        return [
            (source.at[:, where], target.at[:, where], 3 * line + a, here)
            for a, (source, target, where) in enumerate(outside)
        ]

    def loads(slot, lines):
        here = pl.ds(slot, 1)
        copies = [pltpu.make_async_copy(qg_in.at[:, here], qg.at[:, here], load_sem.at[slot, 9])]
        for line in range(lines):
            for source, _, place, here in pieces(slot, line):
                copies.append(
                    pltpu.make_async_copy(source, kv.at[place, :, here], load_sem.at[slot, place])
                )
        return copies

    def stores(slot, line):
        return [
            pltpu.make_async_copy(part.at[place, :, here], target, store_sem.at[slot, place])
            for _, target, place, here in pieces(slot, line)
        ]

    def dq_store(slot):
        here = pl.ds(slot, 1)
        return pltpu.make_async_copy(dq.at[:, here], dq_out.at[:, here], store_sem.at[slot, 9])

    order = [(slot, 1) for slot in range(full, slots)] + [(slot, 3) for slot in range(full)]
    for slot, lines in order:
        for copy in loads(slot, lines):
            copy.start()

    def over_rows(slot, lines, step, after=None):
        def one_line(line, carry):
            start = 3 * line
            here = [valid[slot, start + a] for a in range(3)]
            whole = here[0] * here[1] * here[2]

            @pl.when(whole != 0)
            def _():
                step(start, 3)

            @pl.when(whole == 0)
            def _():
                def one_place(a, carry):
                    @pl.when(valid[slot, start + a] != 0)
                    def _():
                        step(start + a, 1)

                    return carry

                lax.fori_loop(0, 3, one_place, 0)

            if after is not None:
                after(line)
            return carry

        lax.fori_loop(0, lines, one_line, 0)

    def one_slot(slot, lines):
        for copy in loads(slot, lines):
            copy.wait()
        query = qg[:, slot, 0].reshape(tile, head_dim)
        grad = qg[:, slot, 1].reshape(tile, head_dim)
        top[...] = jnp.full(top.shape, -1e30, jnp.float32)
        total[...] = jnp.zeros(total.shape, jnp.float32)
        weighted[...] = jnp.zeros(weighted.shape, jnp.float32)
        dq_t[...] = jnp.zeros(dq_t.shape, jnp.float32)

        def forward(start, count):
            near = pl.ds(start, count)
            key = kv[near, :, slot, 0].reshape(count * tile, head_dim)
            value = kv[near, :, slot, 1].reshape(count * tile, head_dim)
            raw = lax.dot_general(key, query, contract_last, preferred_element_type=jnp.float32)
            rise = lax.dot_general(value, grad, contract_last, preferred_element_type=jnp.float32)
            score[near] = raw.reshape(count, tile, tile)
            dprob[near] = rise.reshape(count, tile, tile)
            top_old = top[...]
            top_new = jnp.maximum(top_old, jnp.max(raw, axis=0, keepdims=True))
            fade = jnp.exp2((top_old - top_new) * to_log2)
            spread = jnp.exp2((raw - top_new) * to_log2)
            top[...] = top_new
            total[...] = total[...] * fade + jnp.sum(spread, axis=0, keepdims=True)
            weighted[...] = weighted[...] * fade + jnp.sum(spread * rise, axis=0, keepdims=True)

        over_rows(slot, lines, forward)
        log_total = top[...] * to_log2 + jnp.log(total[...]) * log2_e
        delta = weighted[...] / total[...]

        def backward(start, count):
            near = pl.ds(start, count)
            key = kv[near, :, slot, 0].reshape(count * tile, head_dim)
            raw = score[near].reshape(count * tile, tile)
            rise = dprob[near].reshape(count * tile, tile)
            prob = jnp.exp2(raw * to_log2 - log_total)
            weight = prob.astype(jnp.bfloat16)
            dscore = (prob * (rise - delta)).astype(jnp.bfloat16)
            dv = jnp.dot(weight, grad, preferred_element_type=jnp.float32)
            dk = jnp.dot(dscore, query, preferred_element_type=jnp.float32) * scale
            dq_t[...] += jnp.dot(key.T, dscore, preferred_element_type=jnp.float32)
            shape = (count, chunks, rows, head_dim)
            part[near, :, slot, 0] = dk.astype(jnp.bfloat16).reshape(shape)
            part[near, :, slot, 1] = dv.astype(jnp.bfloat16).reshape(shape)

        def store_line(line):
            for known in range(lines):

                @pl.when(line == known)
                def _():
                    for copy in stores(slot, known):
                        copy.start()

        over_rows(slot, lines, backward, store_line)
        dq_here = (dq_t[...] * scale).T.astype(jnp.bfloat16)
        dq[:, slot, 0] = dq_here.reshape(chunks, rows, head_dim)
        dq_store(slot).start()

    def tail_slot(slot, carry):
        one_slot(slot, 1)
        return carry

    def full_slot(slot, carry):
        one_slot(slot, 3)
        return carry

    if full < slots:
        lax.fori_loop(full, slots, tail_slot, 0)
    lax.fori_loop(0, full, full_slot, 0)
    for slot, lines in order:
        for line in range(lines):
            for copy in stores(slot, line):
                copy.wait()
        dq_store(slot).wait()


def attend(valid, qg, own, first, second, full):
    chunks, slots, _, rows, _ = qg.shape
    tile = chunks * rows
    bf16, f32 = jnp.bfloat16, jnp.float32
    units = 9 * full + 3 * (slots - full)
    near = [own, *first, *second]
    dq_shape = (chunks, slots, 1, rows, head_dim)
    outs = pl.pallas_call(
        functools.partial(attend_kernel, full),
        out_shape=[jax.ShapeDtypeStruct(dq_shape, bf16)]
        + [jax.ShapeDtypeStruct(array.shape, bf16) for array in near],
        in_specs=[smem_spec] + [hbm_spec] * 6,
        out_specs=[hbm_spec] * 6,
        scratch_shapes=[
            pltpu.VMEM(qg.shape, bf16),
            pltpu.VMEM((9,) + own.shape, bf16),
            pltpu.VMEM((9, tile, tile), f32),
            pltpu.VMEM((9, tile, tile), f32),
            pltpu.VMEM((9,) + own.shape, bf16),
            pltpu.VMEM(dq_shape, bf16),
            pltpu.VMEM((1, tile), f32),
            pltpu.VMEM((1, tile), f32),
            pltpu.VMEM((1, tile), f32),
            pltpu.VMEM((head_dim, tile), f32),
            pltpu.SemaphoreType.DMA((slots, 10)),
            pltpu.SemaphoreType.DMA((slots, 10)),
        ],
        compiler_params=pltpu.CompilerParams(vmem_limit_bytes=attend_vmem),
        cost_estimate=pl.CostEstimate(
            flops=units * 10 * tile * tile * head_dim,
            bytes_accessed=8 * 1024 * 1024,
            transcendentals=units * 2 * tile * tile,
        ),
    )(valid, qg, *near)
    return outs[0], outs[1], outs[2:4], outs[4:6]


def relay_kernel(valid, *refs):
    second, first, out = refs[0:2], refs[2:4], refs[4:6]
    full = out[0].shape[1]
    slots = first[0].shape[1] - 2 * full
    for b in range(2):
        for slot in range(full):
            total = second[b][:, slot].astype(jnp.float32)
            for a in range(2):
                arrived = first[a][:, slots + b * full + slot].astype(jnp.float32)
                total += jnp.where(valid[slot, 3 * b + 4 + a] != 0, arrived, 0.0)
            out[b][:, slot] = total.astype(out[b].dtype)


def relay(valid, second, first):
    return pl.pallas_call(
        relay_kernel,
        out_shape=[jax.ShapeDtypeStruct(array.shape, array.dtype) for array in second],
        in_specs=[smem_spec] + [vmem_spec] * 4,
        compiler_params=small_params,
    )(valid, *second, *first)


def combine_kernel(valid, dq, own, *refs):
    first, second, out = refs[0:2], refs[2:4], refs[4]
    full = second[0].shape[1]
    for slot in range(out.shape[1]):
        total = own[:, slot].astype(jnp.float32)
        for a in range(2):
            arrived = first[a][:, slot].astype(jnp.float32)
            total += jnp.where(valid[slot, a + 1] != 0, arrived, 0.0)
        if slot < full:
            for b in range(2):
                arrived = second[b][:, slot].astype(jnp.float32)
                total += jnp.where(valid[slot, 3 * b + 3] != 0, arrived, 0.0)
        out[:, slot, 0] = dq[:, slot, 0]
        out[:, slot, 1:3] = total.astype(out.dtype)


def combine(valid, dq, own, first, second):
    chunks, slots, _, rows, _ = own.shape
    return pl.pallas_call(
        combine_kernel,
        out_shape=jax.ShapeDtypeStruct((chunks, slots, 3, rows, head_dim), own.dtype),
        in_specs=[smem_spec] + [vmem_spec] * 6,
        out_specs=vmem_spec,
        compiler_params=small_params,
    )(valid, dq, own, *first, *second)


def swap(blocks):
    return lax.all_to_all(blocks, "ta", split_axis=0, concat_axis=0, tiled=True)


def both_kinds(arrays, which):
    swapped = {kind: exchange(arrays[kind - 1], which, kind) for kind in (2, 1)}
    return [swapped[1], swapped[2]]


def with_corners(full, valid, kv, qg):
    kv_full = lax.slice_in_dim(kv, 0, full, axis=1)
    second = [exchange(kv_full, 2, kind) for kind in (1, 2)]
    qg, second[0] = lax.optimization_barrier((qg, second[0]))
    qg = swap(qg)
    message = jnp.concatenate([kv, *second], axis=1)
    first = [exchange(message, 1, kind) for kind in (1, 2)]
    dq, own, first, second = attend(valid, qg, kv, first, second, full)
    first = both_kinds(first, 1)
    second = both_kinds(relay(valid, second, first), 2)
    return combine(valid, dq, own, first, second)


def place_heads(devices, shape, windows, order, valid, choice):
    heads = windows.shape[0]
    slots, half = heads // devices, devices // 2
    kinds = []
    for head in range(heads):
        tall = lax.shift_right_logical(windows[head, 0] - 1, 1)
        wide = lax.shift_right_logical(windows[head, 1] - 1, 1)
        kinds.append(2 * tall + wide)

    def count(kind):
        return functools.reduce(
            lambda a, b: a + b, [(other == kind).astype(jnp.int32) for other in kinds]
        )

    both, rows_only, cols_only = count(3), count(2), count(1)

    def over(count, room):
        return jnp.maximum(count - room, 0)

    chosen = jnp.int32(slots - 1)
    for full in range(slots - 1, 0, -1):
        room = half * (slots - full)
        needed = both + over(rows_only, room) + over(cols_only, room)
        chosen = jnp.where(needed <= devices * full, full - 1, chosen)
    choice[0] = chosen
    full = chosen + 1
    room = half * (slots - full)
    used = both + over(rows_only, room) + over(cols_only, room)
    free = devices * full - used
    rows_used, cols_used = jnp.minimum(rows_only, room), jnp.minimum(cols_only, room)
    rows_free = room - rows_used

    def single(nth, odd):
        return devices * full + devices * lax.div(nth, half) + 2 * lax.rem(nth, half) + odd

    seen = [jnp.int32(0)] * 4
    for head in range(heads):
        kind = kinds[head]
        at = [None] * 4
        at[3] = seen[3]
        at[2] = jnp.where(seen[2] < room, single(seen[2], 0), both + seen[2] - room)
        at[1] = jnp.where(
            seen[1] < room,
            single(seen[1], 1),
            both + over(rows_only, room) + seen[1] - room,
        )
        at[0] = jnp.where(
            seen[0] < free,
            used + seen[0],
            jnp.where(
                seen[0] < free + rows_free,
                single(rows_used + seen[0] - free, 0),
                single(cols_used + seen[0] - free - rows_free, 1),
            ),
        )
        place = at[0]
        for other in range(1, 4):
            place = jnp.where(kind == other, at[other], place)
        order[place] = jnp.int32(head)
        for other in range(4):
            seen[other] = seen[other] + (kind == other).astype(jnp.int32)

    part, row, col = (lax.axis_index(name) for name in ("ta", "ha", "wa"))
    by_rows = lax.rem(part, 2) == 0

    def inside(kind, index, count):
        if kind == 0:
            return jnp.int32(1)
        partner = index ^ 1 if kind == 1 else ((index + 1) ^ 1) - 1
        return ((partner >= 0) & (partner < count)).astype(jnp.int32)

    in_rows = [inside(kind, row, shape[0]) for kind in range(3)]
    in_cols = [inside(kind, col, shape[1]) for kind in range(3)]
    for slot in range(slots):
        head = order[slot * devices + part]
        tall = lax.shift_right_logical(windows[head, 0] - 1, 1)
        wide = lax.shift_right_logical(windows[head, 1] - 1, 1)
        along_rows = [in_rows[0], in_rows[1] * tall, in_rows[2] * tall]
        along_cols = [in_cols[0], in_cols[1] * wide, in_cols[2] * wide]
        for b in range(3):
            for a in range(3):
                valid[slot, 3 * b + a] = jnp.where(
                    by_rows, along_rows[a] * along_cols[b], along_cols[a] * along_rows[b]
                )


def pack_kernel(order, first, second, packed):
    devices, slots = packed.shape[:2]
    for rank in range(devices * slots):
        column = pl.multiple_of(order[rank] * head_dim, head_dim)
        for n, source in enumerate((first, second)):
            packed[rank % devices, rank // devices, n] = source[:, pl.ds(column, head_dim)]


def prepare_kernel(shape, windows, *refs):
    sources, (order, valid, choice, kv) = refs[:2], refs[2:]
    place_heads(kv.shape[0], shape, windows, order, valid, choice)
    pack_kernel(order, *sources, kv)


def on_device(query_tokens, key_tokens, value_tokens, grad_output, windows):
    devices = lax.axis_size("ta")
    heads = windows.shape[0]
    slots = heads // devices
    tokens, features = query_tokens.shape[-2:]
    block = jax.ShapeDtypeStruct((devices, slots, 2, tokens, head_dim), query_tokens.dtype)
    arrays = (key_tokens, value_tokens, query_tokens, grad_output)
    arrays = [array.reshape(tokens, features) for array in arrays]
    shape = (lax.axis_size("ha"), lax.axis_size("wa"))
    order, valid, choice, kv = pl.pallas_call(
        functools.partial(prepare_kernel, shape),
        out_shape=[
            jax.ShapeDtypeStruct((heads,), jnp.int32),
            jax.ShapeDtypeStruct((slots, 9), jnp.int32),
            jax.ShapeDtypeStruct((1,), jnp.int32),
            block,
        ],
        in_specs=[smem_spec] + [vmem_spec] * 2,
        out_specs=[smem_spec] * 3 + [vmem_spec],
        compiler_params=small_params,
    )(windows, *arrays[:2])
    qg = pl.pallas_call(
        pack_kernel,
        out_shape=block,
        in_specs=[smem_spec] + [vmem_spec] * 2,
        out_specs=vmem_spec,
        compiler_params=small_params,
    )(order, *arrays[2:])
    kv = swap(kv)
    branches = [functools.partial(with_corners, full) for full in range(1, slots + 1)]
    outs = unpack(order, swap(lax.switch(choice[0], branches, valid, kv, qg)))
    return tuple(out.reshape(query_tokens.shape) for out in outs)


def solution(mesh):
    shares = P("ha", "wa", "ta", None)
    return jax.shard_map(
        on_device,
        mesh=mesh,
        in_specs=(shares, shares, shares, shares, P()),
        out_specs=(shares, shares, shares),
        check_vma=False,
    )
```

```python
import functools

import jax
import jax.numpy as jnp
import numpy as np
from jax import lax
from jax.experimental import pallas as pl
from jax.experimental.pallas import tpu as pltpu
from jax.sharding import PartitionSpec as P

head_dim = 128
log2_e = 1.4426950408889634
contract_last = (((1,), (1,)), ((), ()))
small_vmem = 12 * 1024 * 1024
attend_vmem = 44 * 1024 * 1024
hbm_spec = pl.BlockSpec(memory_space=pltpu.HBM)
vmem_spec = pl.BlockSpec(memory_space=pltpu.VMEM)
smem_spec = pl.BlockSpec(memory_space=pltpu.SMEM)
small_params = pltpu.CompilerParams(vmem_limit_bytes=small_vmem)


def pair_partner(kind, index, count):
    partner = index ^ 1 if kind == 1 else ((index + 1) ^ 1) - 1
    return partner if 0 <= partner < count else None


def exchange(value, which, kind):
    parts, rows, cols = (lax.axis_size(name) for name in ("ta", "ha", "wa"))
    pairs = []
    for part in range(parts):
        along_rows = (part % 2 == 0) == (which == 1)
        for row in range(rows):
            for col in range(cols):
                to_row, to_col = row, col
                if along_rows:
                    to_row = pair_partner(kind, row, rows)
                else:
                    to_col = pair_partner(kind, col, cols)
                if to_row is not None and to_col is not None:
                    pairs.append(
                        ((part * rows + row) * cols + col, (part * rows + to_row) * cols + to_col)
                    )
    return lax.ppermute(value, ("ta", "ha", "wa"), pairs)


def unpack_kernel(order, packed, *targets):
    devices, slots = packed.shape[:2]
    for rank in range(devices * slots):
        column = pl.multiple_of(order[rank] * head_dim, head_dim)
        for place, target in enumerate(targets):
            target[:, pl.ds(column, head_dim)] = packed[rank % devices, rank // devices, place]


def unpack(order, packed):
    devices, slots, count, tokens, _ = packed.shape
    flat = jax.ShapeDtypeStruct((tokens, devices * slots * head_dim), packed.dtype)
    return pl.pallas_call(
        unpack_kernel,
        out_shape=[flat] * count,
        in_specs=[smem_spec, vmem_spec],
        compiler_params=small_params,
    )(order, packed)


def attend_kernel(full, valid, *refs):
    qg_in, own_in, first_in, second_in = refs[0], refs[1], refs[2:4], refs[4:6]
    dq_out, own_out, first_out, second_out = refs[6], refs[7], refs[8:10], refs[10:12]
    (qg, kv, score, dprob, part, dq, top, top_then, total, weighted, dq_t) = refs[12:23]
    load_sem, store_sem = refs[23:]
    chunks, slots, _, rows, _ = qg.shape
    tile = chunks * rows
    scale = head_dim ** (-0.5)
    to_log2 = scale * log2_e

    def pieces(slot, line):
        here = pl.ds(slot, 1)
        if line == 0:
            outside = [(own_in, own_out, here)]
            outside += [(first_in[a], first_out[a], here) for a in range(2)]
        else:
            passed = pl.ds(slots + (line - 1) * full + slot, 1)
            outside = [(second_in[line - 1], second_out[line - 1], here)]
            outside += [(first_in[a], first_out[a], passed) for a in range(2)]
        return [
            (source.at[:, where], target.at[:, where], 3 * line + a, here)
            for a, (source, target, where) in enumerate(outside)
        ]

    def loads(slot, lines):
        here = pl.ds(slot, 1)
        copies = [pltpu.make_async_copy(qg_in.at[:, here], qg.at[:, here], load_sem.at[slot, 9])]
        for line in range(lines):
            for source, _, place, here in pieces(slot, line):
                copies.append(
                    pltpu.make_async_copy(source, kv.at[place, :, here], load_sem.at[slot, place])
                )
        return copies

    def stores(slot, line):
        return [
            pltpu.make_async_copy(part.at[place, :, here], target, store_sem.at[slot, place])
            for _, target, place, here in pieces(slot, line)
        ]

    def dq_store(slot):
        here = pl.ds(slot, 1)
        return pltpu.make_async_copy(dq.at[:, here], dq_out.at[:, here], store_sem.at[slot, 9])

    order = [(slot, 1) for slot in range(full, slots)] + [(slot, 3) for slot in range(full)]
    for slot, lines in order:
        for copy in loads(slot, lines):
            copy.start()

    def over_rows(slot, lines, step, after=None):
        def one_line(line, carry):
            start = 3 * line
            here = [valid[slot, start + a] for a in range(3)]
            whole = here[0] * here[1] * here[2]

            @pl.when(whole != 0)
            def _():
                step(start, 3)

            @pl.when(whole == 0)
            def _():
                def one_place(a, carry):
                    @pl.when(valid[slot, start + a] != 0)
                    def _():
                        step(start + a, 1)

                    return carry

                lax.fori_loop(0, 3, one_place, 0)

            if after is not None:
                after(line)
            return carry

        lax.fori_loop(0, lines, one_line, 0)

    def one_slot(slot, lines):
        for copy in loads(slot, lines):
            copy.wait()
        query = qg[:, slot, 0].reshape(tile, head_dim)
        grad = qg[:, slot, 1].reshape(tile, head_dim)
        top[...] = jnp.full(top.shape, -1e30, jnp.float32)
        total[...] = jnp.zeros(total.shape, jnp.float32)
        weighted[...] = jnp.zeros(weighted.shape, jnp.float32)
        dq_t[...] = jnp.zeros(dq_t.shape, jnp.float32)

        def forward(start, count):
            near = pl.ds(start, count)
            key = kv[near, :, slot, 0].reshape(count * tile, head_dim)
            value = kv[near, :, slot, 1].reshape(count * tile, head_dim)
            raw = lax.dot_general(key, query, contract_last, preferred_element_type=jnp.float32)
            rise = lax.dot_general(value, grad, contract_last, preferred_element_type=jnp.float32)
            dprob[near] = rise.reshape(count, tile, tile)
            top_old = top[...]
            top_new = jnp.maximum(top_old, jnp.max(raw, axis=0, keepdims=True))
            fade = jnp.exp2((top_old - top_new) * to_log2)
            spread = jnp.exp2((raw - top_new) * to_log2)
            score[near] = spread.reshape(count, tile, tile)
            top[...] = top_new
            top_then[start] = top_new
            total[...] = total[...] * fade + jnp.sum(spread, axis=0, keepdims=True)
            weighted[...] = weighted[...] * fade + jnp.sum(spread * rise, axis=0, keepdims=True)

        over_rows(slot, lines, forward)
        inverse = 1.0 / total[...]
        delta = weighted[...] * inverse

        def backward(start, count):
            near = pl.ds(start, count)
            key = kv[near, :, slot, 0].reshape(count * tile, head_dim)
            rise = dprob[near].reshape(count * tile, tile)
            factor = jnp.exp2((top_then[start] - top[...]) * to_log2) * inverse
            prob = score[near].reshape(count * tile, tile) * factor
            weight = prob.astype(jnp.bfloat16)
            dscore = (prob * (rise - delta)).astype(jnp.bfloat16)
            dv = jnp.dot(weight, grad, preferred_element_type=jnp.float32)
            dk = jnp.dot(dscore, query, preferred_element_type=jnp.float32) * scale
            dq_t[...] += jnp.dot(key.T, dscore, preferred_element_type=jnp.float32)
            shape = (count, chunks, rows, head_dim)
            part[near, :, slot, 0] = dk.astype(jnp.bfloat16).reshape(shape)
            part[near, :, slot, 1] = dv.astype(jnp.bfloat16).reshape(shape)

        def store_line(line):
            for known in range(lines):

                @pl.when(line == known)
                def _():
                    for copy in stores(slot, known):
                        copy.start()

        over_rows(slot, lines, backward, store_line)
        dq_here = (dq_t[...] * scale).T.astype(jnp.bfloat16)
        dq[:, slot, 0] = dq_here.reshape(chunks, rows, head_dim)
        dq_store(slot).start()

    def tail_slot(slot, carry):
        one_slot(slot, 1)
        return carry

    def full_slot(slot, carry):
        one_slot(slot, 3)
        return carry

    if full < slots:
        lax.fori_loop(full, slots, tail_slot, 0)
    lax.fori_loop(0, full, full_slot, 0)
    for slot, lines in order:
        for line in range(lines):
            for copy in stores(slot, line):
                copy.wait()
        dq_store(slot).wait()


def attend(valid, qg, own, first, second, full):
    chunks, slots, _, rows, _ = qg.shape
    tile = chunks * rows
    bf16, f32 = jnp.bfloat16, jnp.float32
    units = 9 * full + 3 * (slots - full)
    near = [own, *first, *second]
    dq_shape = (chunks, slots, 1, rows, head_dim)
    outs = pl.pallas_call(
        functools.partial(attend_kernel, full),
        out_shape=[jax.ShapeDtypeStruct(dq_shape, bf16)]
        + [jax.ShapeDtypeStruct(array.shape, bf16) for array in near],
        in_specs=[smem_spec] + [hbm_spec] * 6,
        out_specs=[hbm_spec] * 6,
        scratch_shapes=[
            pltpu.VMEM(qg.shape, bf16),
            pltpu.VMEM((9,) + own.shape, bf16),
            pltpu.VMEM((9, tile, tile), f32),
            pltpu.VMEM((9, tile, tile), f32),
            pltpu.VMEM((9,) + own.shape, bf16),
            pltpu.VMEM(dq_shape, bf16),
            pltpu.VMEM((1, tile), f32),
            pltpu.VMEM((9, 1, tile), f32),
            pltpu.VMEM((1, tile), f32),
            pltpu.VMEM((1, tile), f32),
            pltpu.VMEM((head_dim, tile), f32),
            pltpu.SemaphoreType.DMA((slots, 10)),
            pltpu.SemaphoreType.DMA((slots, 10)),
        ],
        compiler_params=pltpu.CompilerParams(vmem_limit_bytes=attend_vmem),
        cost_estimate=pl.CostEstimate(
            flops=units * 10 * tile * tile * head_dim,
            bytes_accessed=8 * 1024 * 1024,
            transcendentals=units * 2 * tile * tile,
        ),
    )(valid, qg, *near)
    return outs[0], outs[1], outs[2:4], outs[4:6]


def join_kernel(*refs):
    out, start = refs[-1], 0
    for part in refs[:-1]:
        out[:, start : start + part.shape[1]] = part[...]
        start += part.shape[1]


def join(parts):
    chunks, _, *rest = parts[0].shape
    slots = sum(part.shape[1] for part in parts)
    return pl.pallas_call(
        join_kernel,
        out_shape=jax.ShapeDtypeStruct((chunks, slots, *rest), parts[0].dtype),
        in_specs=[vmem_spec] * len(parts),
        out_specs=vmem_spec,
        compiler_params=small_params,
    )(*parts)


def relay_kernel(valid, *refs):
    second, first, out = refs[0:2], refs[2:4], refs[4:6]
    full = out[0].shape[1]
    slots = first[0].shape[1] - 2 * full
    for b in range(2):
        for slot in range(full):
            total = second[b][:, slot].astype(jnp.float32)
            for a in range(2):
                arrived = first[a][:, slots + b * full + slot].astype(jnp.float32)
                total += jnp.where(valid[slot, 3 * b + 4 + a] != 0, arrived, 0.0)
            out[b][:, slot] = total.astype(out[b].dtype)


def relay(valid, second, first):
    return pl.pallas_call(
        relay_kernel,
        out_shape=[jax.ShapeDtypeStruct(array.shape, array.dtype) for array in second],
        in_specs=[smem_spec] + [vmem_spec] * 4,
        compiler_params=small_params,
    )(valid, *second, *first)


def combine_kernel(valid, dq, own, *refs):
    first, second, out = refs[0:2], refs[2:4], refs[4]
    full = second[0].shape[1]
    for slot in range(out.shape[1]):
        total = own[:, slot].astype(jnp.float32)
        for a in range(2):
            arrived = first[a][:, slot].astype(jnp.float32)
            total += jnp.where(valid[slot, a + 1] != 0, arrived, 0.0)
        if slot < full:
            for b in range(2):
                arrived = second[b][:, slot].astype(jnp.float32)
                total += jnp.where(valid[slot, 3 * b + 3] != 0, arrived, 0.0)
        out[:, slot, 0] = dq[:, slot, 0]
        out[:, slot, 1:3] = total.astype(out.dtype)


def combine(valid, dq, own, first, second):
    chunks, slots, _, rows, _ = own.shape
    return pl.pallas_call(
        combine_kernel,
        out_shape=jax.ShapeDtypeStruct((chunks, slots, 3, rows, head_dim), own.dtype),
        in_specs=[smem_spec] + [vmem_spec] * 6,
        out_specs=vmem_spec,
        compiler_params=small_params,
    )(valid, dq, own, *first, *second)


def swap(blocks):
    return lax.all_to_all(blocks, "ta", split_axis=0, concat_axis=0, tiled=True)


def both_kinds(arrays, which):
    swapped = {kind: exchange(arrays[kind - 1], which, kind) for kind in (2, 1)}
    return [swapped[1], swapped[2]]


def with_corners(full, valid, kv, qg):
    kv_full = lax.slice_in_dim(kv, 0, full, axis=1)
    second = [exchange(kv_full, 2, kind) for kind in (1, 2)]
    qg, second[0] = lax.optimization_barrier((qg, second[0]))
    qg = swap(qg)
    message = join([kv, *second])
    first = [exchange(message, 1, kind) for kind in (1, 2)]
    dq, own, first, second = attend(valid, qg, kv, first, second, full)
    first = both_kinds(first, 1)
    second = both_kinds(relay(valid, second, first), 2)
    return combine(valid, dq, own, first, second)


def place_heads(devices, shape, windows, order, valid, choice):
    heads = windows.shape[0]
    slots, half = heads // devices, devices // 2
    kinds = []
    for head in range(heads):
        tall = lax.shift_right_logical(windows[head, 0] - 1, 1)
        wide = lax.shift_right_logical(windows[head, 1] - 1, 1)
        kinds.append(2 * tall + wide)

    def count(kind):
        return functools.reduce(
            lambda a, b: a + b, [(other == kind).astype(jnp.int32) for other in kinds]
        )

    both, rows_only, cols_only = count(3), count(2), count(1)

    def over(count, room):
        return jnp.maximum(count - room, 0)

    chosen = jnp.int32(slots - 1)
    for full in range(slots - 1, 0, -1):
        room = half * (slots - full)
        needed = both + over(rows_only, room) + over(cols_only, room)
        chosen = jnp.where(needed <= devices * full, full - 1, chosen)
    choice[0] = chosen
    full = chosen + 1
    room = half * (slots - full)
    used = both + over(rows_only, room) + over(cols_only, room)
    free = devices * full - used
    rows_used, cols_used = jnp.minimum(rows_only, room), jnp.minimum(cols_only, room)
    rows_free = room - rows_used

    def single(nth, odd):
        return devices * full + devices * lax.div(nth, half) + 2 * lax.rem(nth, half) + odd

    seen = [jnp.int32(0)] * 4
    for head in range(heads):
        kind = kinds[head]
        at = [None] * 4
        at[3] = seen[3]
        at[2] = jnp.where(seen[2] < room, single(seen[2], 0), both + seen[2] - room)
        at[1] = jnp.where(
            seen[1] < room,
            single(seen[1], 1),
            both + over(rows_only, room) + seen[1] - room,
        )
        at[0] = jnp.where(
            seen[0] < free,
            used + seen[0],
            jnp.where(
                seen[0] < free + rows_free,
                single(rows_used + seen[0] - free, 0),
                single(cols_used + seen[0] - free - rows_free, 1),
            ),
        )
        place = at[0]
        for other in range(1, 4):
            place = jnp.where(kind == other, at[other], place)
        order[place] = jnp.int32(head)
        for other in range(4):
            seen[other] = seen[other] + (kind == other).astype(jnp.int32)

    part, row, col = (lax.axis_index(name) for name in ("ta", "ha", "wa"))
    by_rows = lax.rem(part, 2) == 0

    def inside(kind, index, count):
        if kind == 0:
            return jnp.int32(1)
        partner = index ^ 1 if kind == 1 else ((index + 1) ^ 1) - 1
        return ((partner >= 0) & (partner < count)).astype(jnp.int32)

    in_rows = [inside(kind, row, shape[0]) for kind in range(3)]
    in_cols = [inside(kind, col, shape[1]) for kind in range(3)]
    for slot in range(slots):
        head = order[slot * devices + part]
        tall = lax.shift_right_logical(windows[head, 0] - 1, 1)
        wide = lax.shift_right_logical(windows[head, 1] - 1, 1)
        along_rows = [in_rows[0], in_rows[1] * tall, in_rows[2] * tall]
        along_cols = [in_cols[0], in_cols[1] * wide, in_cols[2] * wide]
        for b in range(3):
            for a in range(3):
                valid[slot, 3 * b + a] = jnp.where(
                    by_rows, along_rows[a] * along_cols[b], along_cols[a] * along_rows[b]
                )


def pack_kernel(order, first, second, packed):
    devices, slots = packed.shape[:2]
    for rank in range(devices * slots):
        column = pl.multiple_of(order[rank] * head_dim, head_dim)
        for n, source in enumerate((first, second)):
            packed[rank % devices, rank // devices, n] = source[:, pl.ds(column, head_dim)]


def prepare_kernel(shape, windows, *refs):
    sources, (order, valid, choice, kv) = refs[:2], refs[2:]
    place_heads(kv.shape[0], shape, windows, order, valid, choice)
    pack_kernel(order, *sources, kv)


def on_device(query_tokens, key_tokens, value_tokens, grad_output, windows):
    devices = lax.axis_size("ta")
    heads = windows.shape[0]
    slots = heads // devices
    tokens, features = query_tokens.shape[-2:]
    block = jax.ShapeDtypeStruct((devices, slots, 2, tokens, head_dim), query_tokens.dtype)
    arrays = (key_tokens, value_tokens, query_tokens, grad_output)
    arrays = [array.reshape(tokens, features) for array in arrays]
    shape = (lax.axis_size("ha"), lax.axis_size("wa"))
    order, valid, choice, kv = pl.pallas_call(
        functools.partial(prepare_kernel, shape),
        out_shape=[
            jax.ShapeDtypeStruct((heads,), jnp.int32),
            jax.ShapeDtypeStruct((slots, 9), jnp.int32),
            jax.ShapeDtypeStruct((1,), jnp.int32),
            block,
        ],
        in_specs=[smem_spec] + [vmem_spec] * 2,
        out_specs=[smem_spec] * 3 + [vmem_spec],
        compiler_params=small_params,
    )(windows, *arrays[:2])
    qg = pl.pallas_call(
        pack_kernel,
        out_shape=block,
        in_specs=[smem_spec] + [vmem_spec] * 2,
        out_specs=vmem_spec,
        compiler_params=small_params,
    )(order, *arrays[2:])
    kv = swap(kv)
    branches = [functools.partial(with_corners, full) for full in range(1, slots + 1)]
    outs = unpack(order, swap(lax.switch(choice[0], branches, valid, kv, qg)))
    return tuple(out.reshape(query_tokens.shape) for out in outs)


def solution(mesh):
    shares = P("ha", "wa", "ta", None)
    return jax.shard_map(
        on_device,
        mesh=mesh,
        in_specs=(shares, shares, shares, shares, P()),
        out_specs=(shares, shares, shares),
        check_vma=False,
    )
```

```python
import functools

import jax
import jax.numpy as jnp
import numpy as np
from jax import lax
from jax.experimental import pallas as pl
from jax.experimental.pallas import tpu as pltpu
from jax.sharding import PartitionSpec as P

head_dim = 128
log2_e = 1.4426950408889634
contract_last = (((1,), (1,)), ((), ()))
small_vmem = 12 * 1024 * 1024
attend_vmem = 44 * 1024 * 1024
whole_vmem = 60 * 1024 * 1024
hbm_spec = pl.BlockSpec(memory_space=pltpu.HBM)
vmem_spec = pl.BlockSpec(memory_space=pltpu.VMEM)
smem_spec = pl.BlockSpec(memory_space=pltpu.SMEM)
small_params = pltpu.CompilerParams(vmem_limit_bytes=small_vmem)


def pair_partner(kind, index, count):
    partner = index ^ 1 if kind == 1 else ((index + 1) ^ 1) - 1
    return partner if 0 <= partner < count else None


def exchange(value, which, kind):
    parts, rows, cols = (lax.axis_size(name) for name in ("ta", "ha", "wa"))
    pairs = []
    for part in range(parts):
        along_rows = (part % 2 == 0) == (which == 1)
        for row in range(rows):
            for col in range(cols):
                to_row, to_col = row, col
                if along_rows:
                    to_row = pair_partner(kind, row, rows)
                else:
                    to_col = pair_partner(kind, col, cols)
                if to_row is not None and to_col is not None:
                    pairs.append(
                        ((part * rows + row) * cols + col, (part * rows + to_row) * cols + to_col)
                    )
    return lax.ppermute(value, ("ta", "ha", "wa"), pairs)


def unpack_kernel(order, packed, *targets):
    devices, slots = packed.shape[:2]
    for rank in range(devices * slots):
        column = pl.multiple_of(order[rank] * head_dim, head_dim)
        for place, target in enumerate(targets):
            target[:, pl.ds(column, head_dim)] = packed[rank % devices, rank // devices, place]


def unpack(order, packed):
    devices, slots, count, tokens, _ = packed.shape
    flat = jax.ShapeDtypeStruct((tokens, devices * slots * head_dim), packed.dtype)
    return pl.pallas_call(
        unpack_kernel,
        out_shape=[flat] * count,
        in_specs=[smem_spec, vmem_spec],
        compiler_params=small_params,
    )(order, packed)


def attend_kernel(full, valid, *refs):
    qg_in, own_in, first_in, second_in = refs[0], refs[1], refs[2:4], refs[4:6]
    dq_out, own_out, first_out, second_out = refs[6], refs[7], refs[8:10], refs[10:12]
    (qg, kv, score, dprob, part, dq, top, top_then, total, weighted, dq_t) = refs[12:23]
    load_sem, store_sem = refs[23:]
    chunks, slots, _, rows, _ = qg.shape
    tile = chunks * rows
    scale = head_dim ** (-0.5)
    to_log2 = scale * log2_e

    def pieces(slot, line):
        here = pl.ds(slot, 1)
        if line == 0:
            outside = [(own_in, own_out, here)]
            outside += [(first_in[a], first_out[a], here) for a in range(2)]
        else:
            passed = pl.ds(slots + (line - 1) * full + slot, 1)
            outside = [(second_in[line - 1], second_out[line - 1], here)]
            outside += [(first_in[a], first_out[a], passed) for a in range(2)]
        return [
            (source.at[:, where], target.at[:, where], 3 * line + a, here)
            for a, (source, target, where) in enumerate(outside)
        ]

    def loads(slot, lines):
        here = pl.ds(slot, 1)
        copies = [pltpu.make_async_copy(qg_in.at[:, here], qg.at[:, here], load_sem.at[slot, 9])]
        for line in range(lines):
            for source, _, place, here in pieces(slot, line):
                copies.append(
                    pltpu.make_async_copy(source, kv.at[place, :, here], load_sem.at[slot, place])
                )
        return copies

    def stores(slot, line):
        return [
            pltpu.make_async_copy(part.at[place, :, here], target, store_sem.at[slot, place])
            for _, target, place, here in pieces(slot, line)
        ]

    def dq_store(slot):
        here = pl.ds(slot, 1)
        return pltpu.make_async_copy(dq.at[:, here], dq_out.at[:, here], store_sem.at[slot, 9])

    order = [(slot, 1) for slot in range(full, slots)] + [(slot, 3) for slot in range(full)]
    for slot, lines in order:
        for copy in loads(slot, lines):
            copy.start()

    def over_rows(slot, lines, step, after=None):
        def one_line(line, carry):
            start = 3 * line
            here = [valid[slot, start + a] for a in range(3)]
            whole = here[0] * here[1] * here[2]

            @pl.when(whole != 0)
            def _():
                step(start, 3)

            @pl.when(whole == 0)
            def _():
                def one_place(a, carry):
                    @pl.when(valid[slot, start + a] != 0)
                    def _():
                        step(start + a, 1)

                    return carry

                lax.fori_loop(0, 3, one_place, 0)

            if after is not None:
                after(line)
            return carry

        lax.fori_loop(0, lines, one_line, 0)

    def one_slot(slot, lines):
        for copy in loads(slot, lines):
            copy.wait()
        query = qg[:, slot, 0].reshape(tile, head_dim)
        grad = qg[:, slot, 1].reshape(tile, head_dim)
        top[...] = jnp.full(top.shape, -1e30, jnp.float32)
        total[...] = jnp.zeros(total.shape, jnp.float32)
        weighted[...] = jnp.zeros(weighted.shape, jnp.float32)
        dq_t[...] = jnp.zeros(dq_t.shape, jnp.float32)

        def forward(start, count):
            near = pl.ds(start, count)
            key = kv[near, :, slot, 0].reshape(count * tile, head_dim)
            value = kv[near, :, slot, 1].reshape(count * tile, head_dim)
            raw = lax.dot_general(key, query, contract_last, preferred_element_type=jnp.float32)
            rise = lax.dot_general(value, grad, contract_last, preferred_element_type=jnp.float32)
            dprob[near] = rise.reshape(count, tile, tile)
            top_old = top[...]
            top_new = jnp.maximum(top_old, jnp.max(raw, axis=0, keepdims=True))
            fade = jnp.exp2((top_old - top_new) * to_log2)
            spread = jnp.exp2((raw - top_new) * to_log2)
            score[near] = spread.reshape(count, tile, tile)
            top[...] = top_new
            top_then[start] = top_new
            total[...] = total[...] * fade + jnp.sum(spread, axis=0, keepdims=True)
            weighted[...] = weighted[...] * fade + jnp.sum(spread * rise, axis=0, keepdims=True)

        over_rows(slot, lines, forward)
        inverse = 1.0 / total[...]
        delta = weighted[...] * inverse

        def backward(start, count):
            near = pl.ds(start, count)
            key = kv[near, :, slot, 0].reshape(count * tile, head_dim)
            rise = dprob[near].reshape(count * tile, tile)
            factor = jnp.exp2((top_then[start] - top[...]) * to_log2) * inverse
            prob = score[near].reshape(count * tile, tile) * factor
            weight = prob.astype(jnp.bfloat16)
            dscore = (prob * (rise - delta)).astype(jnp.bfloat16)
            dv = jnp.dot(weight, grad, preferred_element_type=jnp.float32)
            dk = jnp.dot(dscore, query, preferred_element_type=jnp.float32) * scale
            dq_t[...] += jnp.dot(key.T, dscore, preferred_element_type=jnp.float32)
            shape = (count, chunks, rows, head_dim)
            part[near, :, slot, 0] = dk.astype(jnp.bfloat16).reshape(shape)
            part[near, :, slot, 1] = dv.astype(jnp.bfloat16).reshape(shape)

        def store_line(line):
            for known in range(lines):

                @pl.when(line == known)
                def _():
                    for copy in stores(slot, known):
                        copy.start()

        over_rows(slot, lines, backward, store_line)
        dq_here = (dq_t[...] * scale).T.astype(jnp.bfloat16)
        dq[:, slot, 0] = dq_here.reshape(chunks, rows, head_dim)
        dq_store(slot).start()

    def tail_slot(slot, carry):
        one_slot(slot, 1)
        return carry

    def full_slot(slot, carry):
        one_slot(slot, 3)
        return carry

    if full < slots:
        lax.fori_loop(full, slots, tail_slot, 0)
    lax.fori_loop(0, full, full_slot, 0)
    for slot, lines in order:
        for line in range(lines):
            for copy in stores(slot, line):
                copy.wait()
        dq_store(slot).wait()


def attend(valid, qg, own, first, second, full):
    chunks, slots, _, rows, _ = qg.shape
    tile = chunks * rows
    bf16, f32 = jnp.bfloat16, jnp.float32
    units = 9 * full + 3 * (slots - full)
    near = [own, *first, *second]
    dq_shape = (chunks, slots, 1, rows, head_dim)
    outs = pl.pallas_call(
        functools.partial(attend_kernel, full),
        out_shape=[jax.ShapeDtypeStruct(dq_shape, bf16)]
        + [jax.ShapeDtypeStruct(array.shape, bf16) for array in near],
        in_specs=[smem_spec] + [hbm_spec] * 6,
        out_specs=[hbm_spec] * 6,
        scratch_shapes=[
            pltpu.VMEM(qg.shape, bf16),
            pltpu.VMEM((9,) + own.shape, bf16),
            pltpu.VMEM((9, tile, tile), f32),
            pltpu.VMEM((9, tile, tile), f32),
            pltpu.VMEM((9,) + own.shape, bf16),
            pltpu.VMEM(dq_shape, bf16),
            pltpu.VMEM((1, tile), f32),
            pltpu.VMEM((9, 1, tile), f32),
            pltpu.VMEM((1, tile), f32),
            pltpu.VMEM((1, tile), f32),
            pltpu.VMEM((head_dim, tile), f32),
            pltpu.SemaphoreType.DMA((slots, 10)),
            pltpu.SemaphoreType.DMA((slots, 10)),
        ],
        compiler_params=pltpu.CompilerParams(vmem_limit_bytes=attend_vmem),
        cost_estimate=pl.CostEstimate(
            flops=units * 10 * tile * tile * head_dim,
            bytes_accessed=8 * 1024 * 1024,
            transcendentals=units * 2 * tile * tile,
        ),
    )(valid, qg, *near)
    return outs[0], outs[1], outs[2:4], outs[4:6]


def join_kernel(*refs):
    out, start = refs[-1], 0
    for part in refs[:-1]:
        out[:, start : start + part.shape[1]] = part[...]
        start += part.shape[1]


def join(parts):
    chunks, _, *rest = parts[0].shape
    slots = sum(part.shape[1] for part in parts)
    return pl.pallas_call(
        join_kernel,
        out_shape=jax.ShapeDtypeStruct((chunks, slots, *rest), parts[0].dtype),
        in_specs=[vmem_spec] * len(parts),
        out_specs=vmem_spec,
        compiler_params=small_params,
    )(*parts)


def relay_kernel(valid, *refs):
    second, first, out = refs[0:2], refs[2:4], refs[4:6]
    full = out[0].shape[1]
    slots = first[0].shape[1] - 2 * full
    for b in range(2):
        for slot in range(full):
            total = second[b][:, slot].astype(jnp.float32)
            for a in range(2):
                arrived = first[a][:, slots + b * full + slot].astype(jnp.float32)
                total += jnp.where(valid[slot, 3 * b + 4 + a] != 0, arrived, 0.0)
            out[b][:, slot] = total.astype(out[b].dtype)


def relay(valid, second, first):
    return pl.pallas_call(
        relay_kernel,
        out_shape=[jax.ShapeDtypeStruct(array.shape, array.dtype) for array in second],
        in_specs=[smem_spec] + [vmem_spec] * 4,
        compiler_params=small_params,
    )(valid, *second, *first)


def combine_kernel(valid, dq, own, *refs):
    first, second, out = refs[0:2], refs[2:4], refs[4]
    full = second[0].shape[1]
    for slot in range(out.shape[1]):
        total = own[:, slot].astype(jnp.float32)
        for a in range(2):
            arrived = first[a][:, slot].astype(jnp.float32)
            total += jnp.where(valid[slot, a + 1] != 0, arrived, 0.0)
        if slot < full:
            for b in range(2):
                arrived = second[b][:, slot].astype(jnp.float32)
                total += jnp.where(valid[slot, 3 * b + 3] != 0, arrived, 0.0)
        out[:, slot, 0] = dq[:, slot, 0]
        out[:, slot, 1:3] = total.astype(out.dtype)


def combine(valid, dq, own, first, second):
    chunks, slots, _, rows, _ = own.shape
    return pl.pallas_call(
        combine_kernel,
        out_shape=jax.ShapeDtypeStruct((chunks, slots, 3, rows, head_dim), own.dtype),
        in_specs=[smem_spec] + [vmem_spec] * 6,
        out_specs=vmem_spec,
        compiler_params=small_params,
    )(valid, dq, own, *first, *second)


def swap(blocks):
    return lax.all_to_all(blocks, "ta", split_axis=0, concat_axis=0, tiled=True)


def both_kinds(arrays, which):
    swapped = {kind: exchange(arrays[kind - 1], which, kind) for kind in (2, 1)}
    return [swapped[1], swapped[2]]


def with_corners(full, valid, kv, qg):
    kv_full = lax.slice_in_dim(kv, 0, full, axis=1)
    second = [exchange(kv_full, 2, kind) for kind in (1, 2)]
    qg, second[0] = lax.optimization_barrier((qg, second[0]))
    qg = swap(qg)
    message = join([kv, *second])
    first = [exchange(message, 1, kind) for kind in (1, 2)]
    dq, own, first, second = attend(valid, qg, kv, first, second, full)
    first = both_kinds(first, 1)
    second = both_kinds(relay(valid, second, first), 2)
    return combine(valid, dq, own, first, second)


def place_heads(devices, shape, windows, order, valid, choice):
    heads = windows.shape[0]
    slots, half = heads // devices, devices // 2
    kinds = []
    for head in range(heads):
        tall = lax.shift_right_logical(windows[head, 0] - 1, 1)
        wide = lax.shift_right_logical(windows[head, 1] - 1, 1)
        kinds.append(2 * tall + wide)

    def count(kind):
        return functools.reduce(
            lambda a, b: a + b, [(other == kind).astype(jnp.int32) for other in kinds]
        )

    both, rows_only, cols_only = count(3), count(2), count(1)

    def over(count, room):
        return jnp.maximum(count - room, 0)

    chosen = jnp.int32(slots - 1)
    for full in range(slots - 1, 0, -1):
        room = half * (slots - full)
        needed = both + over(rows_only, room) + over(cols_only, room)
        chosen = jnp.where(needed <= devices * full, full - 1, chosen)
    choice[0] = chosen
    full = chosen + 1
    room = half * (slots - full)
    used = both + over(rows_only, room) + over(cols_only, room)
    free = devices * full - used
    rows_used, cols_used = jnp.minimum(rows_only, room), jnp.minimum(cols_only, room)
    rows_free = room - rows_used

    def single(nth, odd):
        return devices * full + devices * lax.div(nth, half) + 2 * lax.rem(nth, half) + odd

    seen = [jnp.int32(0)] * 4
    for head in range(heads):
        kind = kinds[head]
        at = [None] * 4
        at[3] = seen[3]
        at[2] = jnp.where(seen[2] < room, single(seen[2], 0), both + seen[2] - room)
        at[1] = jnp.where(
            seen[1] < room,
            single(seen[1], 1),
            both + over(rows_only, room) + seen[1] - room,
        )
        at[0] = jnp.where(
            seen[0] < free,
            used + seen[0],
            jnp.where(
                seen[0] < free + rows_free,
                single(rows_used + seen[0] - free, 0),
                single(cols_used + seen[0] - free - rows_free, 1),
            ),
        )
        place = at[0]
        for other in range(1, 4):
            place = jnp.where(kind == other, at[other], place)
        order[place] = jnp.int32(head)
        for other in range(4):
            seen[other] = seen[other] + (kind == other).astype(jnp.int32)

    part, row, col = (lax.axis_index(name) for name in ("ta", "ha", "wa"))
    by_rows = lax.rem(part, 2) == 0

    def inside(kind, index, count):
        if kind == 0:
            return jnp.int32(1)
        partner = index ^ 1 if kind == 1 else ((index + 1) ^ 1) - 1
        return ((partner >= 0) & (partner < count)).astype(jnp.int32)

    in_rows = [inside(kind, row, shape[0]) for kind in range(3)]
    in_cols = [inside(kind, col, shape[1]) for kind in range(3)]
    for slot in range(slots):
        head = order[slot * devices + part]
        tall = lax.shift_right_logical(windows[head, 0] - 1, 1)
        wide = lax.shift_right_logical(windows[head, 1] - 1, 1)
        along_rows = [in_rows[0], in_rows[1] * tall, in_rows[2] * tall]
        along_cols = [in_cols[0], in_cols[1] * wide, in_cols[2] * wide]
        for b in range(3):
            for a in range(3):
                valid[slot, 3 * b + a] = jnp.where(
                    by_rows, along_rows[a] * along_cols[b], along_cols[a] * along_rows[b]
                )


def pack_kernel(order, first, second, packed):
    devices, slots = packed.shape[:2]
    for rank in range(devices * slots):
        column = pl.multiple_of(order[rank] * head_dim, head_dim)
        for n, source in enumerate((first, second)):
            packed[rank % devices, rank // devices, n] = source[:, pl.ds(column, head_dim)]


def prepare_kernel(shape, windows, *refs):
    sources, (order, valid, choice, kv) = refs[:2], refs[2:]
    place_heads(kv.shape[0], shape, windows, order, valid, choice)
    pack_kernel(order, *sources, kv)


def on_device(query_tokens, key_tokens, value_tokens, grad_output, windows):
    devices = lax.axis_size("ta")
    heads = windows.shape[0]
    slots = heads // devices
    tokens, features = query_tokens.shape[-2:]
    block = jax.ShapeDtypeStruct((devices, slots, 2, tokens, head_dim), query_tokens.dtype)
    arrays = (key_tokens, value_tokens, query_tokens, grad_output)
    arrays = [array.reshape(tokens, features) for array in arrays]
    shape = (lax.axis_size("ha"), lax.axis_size("wa"))
    order, valid, choice, kv = pl.pallas_call(
        functools.partial(prepare_kernel, shape),
        out_shape=[
            jax.ShapeDtypeStruct((heads,), jnp.int32),
            jax.ShapeDtypeStruct((slots, 9), jnp.int32),
            jax.ShapeDtypeStruct((1,), jnp.int32),
            block,
        ],
        in_specs=[smem_spec] + [vmem_spec] * 2,
        out_specs=[smem_spec] * 3 + [vmem_spec],
        compiler_params=pltpu.CompilerParams(vmem_limit_bytes=whole_vmem),
    )(windows, *arrays[:2])
    qg = pl.pallas_call(
        pack_kernel,
        out_shape=block,
        in_specs=[smem_spec] + [vmem_spec] * 2,
        out_specs=vmem_spec,
        compiler_params=small_params,
    )(order, *arrays[2:])
    kv = swap(kv)
    branches = [functools.partial(with_corners, full) for full in range(1, slots + 1)]
    outs = unpack(order, swap(lax.switch(choice[0], branches, valid, kv, qg)))
    return tuple(out.reshape(query_tokens.shape) for out in outs)


def solution(mesh):
    shares = P("ha", "wa", "ta", None)
    return jax.shard_map(
        on_device,
        mesh=mesh,
        in_specs=(shares, shares, shares, shares, P()),
        out_specs=(shares, shares, shares),
        check_vma=False,
    )
```
